128 devices in a mesh: box: 8 (over y, core), dir: 16 (over x, z).
Axes of the slice: x: 4, y: 4, z: 4, core: 2. Of those that a mesh axis runs over, the one named last changes fastest.
Arguments:
- leaf_pattern: float32 [2, 6144, 2048], P(None, ('box', 'dir')), may hold values from -6 to 6
- leaf_parent: int32 [128, 48], P(('box', 'dir')), may hold values from 0 to 7, never falling along the last dimension, each value on 1 to 8 neighbouring positions
- octant: int32 [6144], P(('box', 'dir')), may hold values from 0 to 7
- interp_theta: float32 [64, 32], replicated, may hold values from -1 to 1
- interp_phi: float32 [128, 64], replicated, may hold values from -0.75 to 0.75
- shift_angle: float32 [8, 8192], replicated, may hold values from -3.140625 to 3.140625
- near_src: int32 [6144, 16], P(('box', 'dir')), may hold values from 0 to 6143, as said below
- near_type: int32 [6144, 16], P(('box', 'dir')), may hold values from 0 to 315
- leaf_transfer: float32 [2, 316, 2048], replicated, may hold values from -1 to 1
- inter_src: int32 [1024, 32], P('box'), may hold values from 0 to 1023, as said below
- inter_type: int32 [1024, 32], P('box'), may hold values from 0 to 315
- top_transfer: float32 [2, 316, 8192], P(None, None, 'dir'), may hold values from -0.375 to 0.375
Outputs:
- incoming: float32 [2, 1024, 8192], P(None, 'box', 'dir')
- leaf_incoming: float32 [2, 6144, 2048], P(None, ('box', 'dir'))
The draws below stay inside these ranges and needn't reach their ends.
Inputs may be any that keep to these rules, and one draw needn't show every extreme that they name: `leaf_parent`: along each row the parents never fall, and every parent has 1 to 8 leaves. near_src[i, j] lies within i - 16 to i + 16. inter_src[r, j] lies in box groups r // 128 - 1 to r // 128 + 1, a group being 128 consecutive boxes.
All inputs are finite; a program needn't handle non-finite values.
Results may differ from the reference program's by a relative error of at most 0.0003.
Values sent between devices are 32-bit elements; how exact they have to be, the bound alone decides.
No kernel may reach another device: no remote copies, remote signals or barrier semaphores. Data moves between devices by JAX's collectives and lax.ppermute only.
A program may use at most 192 MiB of HBM per device.

```python
import math
import jax
import jax.numpy as jnp
import numpy as np
from jax import lax

TL = 32
PL = 64
TT = 64
PT = 128
KL = 2048
KT = 8192
PAR_DEV = 8
LEAF_DEV = 48
REACH = 16
GROUP = 128
NT = 1024
NLEAF = 6144
M = 32
MN = 16
NTYPE = 316
DEVICES = 128


def draw_inter_src(key, part):
    key = jax.random.fold_in(key, 11)
    receiver = jnp.arange(NT, dtype=jnp.int32)
    groups = NT // GROUP
    member = receiver // GROUP
    lowest = jnp.maximum(member - 1, 0) * GROUP
    highest = jnp.minimum(member + 2, groups) * GROUP
    picked = jax.random.randint(key, (NT, M), lowest[:, None], highest[:, None], dtype=jnp.int32)
    picked = picked.at[0, 0].set(0)
    picked = picked.at[NT - 1, M - 1].set(NT - 1)
    return picked


def draw_near_src(key, part):
    key = jax.random.fold_in(key, 23)
    leaf_index = jnp.arange(NLEAF, dtype=jnp.int32)
    lowest = jnp.maximum(leaf_index - REACH, 0)
    highest = jnp.minimum(leaf_index + REACH + 1, NLEAF)
    picked = jax.random.randint(key, (NLEAF, MN), lowest[:, None], highest[:, None], dtype=jnp.int32)
    picked = picked.at[0, 0].set(0)
    picked = picked.at[NLEAF - 1, MN - 1].set(NLEAF - 1)
    return picked


def touch_ends(result, key, low, largest):
    longest = result.shape.index(max(result.shape))
    spots = []
    for shift in (0, 1):
        where = [jax.random.randint(jax.random.fold_in(key, axis), (), 0, length) for axis, length in enumerate(result.shape)]
        where[longest] = (where[longest] + shift) % result.shape[longest]
        spots.append(tuple(where))
    return result.at[spots[0]].set(low).at[spots[1]].set(largest)


def block_scale(stream_key, dims, cuts, smallest, top_value):
    level = 1.0
    for axis_at, shards_of in cuts:
        heights = jax.random.uniform(jax.random.fold_in(jax.random.fold_in(stream_key, 6), axis_at), (shards_of,), jnp.float32, smallest / len(cuts), top_value / len(cuts))
        level = level * jnp.repeat(jnp.exp(heights), dims[axis_at] // shards_of).reshape((-1,) + (1,) * (len(dims) - 1 - axis_at))
    return level


def length_profile(number_of, total, reach, slope):
    portions = [(1 << 20) // math.isqrt(rank ** slope) + 1 for rank in range(2, number_of + 1)]
    surplus, given = total - reach - (number_of - 1), [1] * (number_of - 1)
    while surplus > 0:
        candidates = [i for i in range(number_of - 1) if given[i] < reach]
        pool, left = sum([portions[i] for i in candidates]), surplus
        for i in candidates:
            extra = min(reach - given[i], max(1, left * portions[i] // pool), surplus)
            given[i] = given[i] + extra
            surplus = surplus - extra
    return np.array([reach] + given)


def ragged(rng, amount, total, most, skew):
    if amount == 2:
        one = jax.random.randint(rng, (), max(1, total - most), min(most, total - 1) + 1)
        return jnp.stack([one, total - one])
    sizes = jnp.asarray(length_profile(amount, total, most, skew), jnp.int32)
    twos = (amount - 1) // 2
    donor, sink = sizes[1:1 + 2 * twos:2], sizes[2:2 + 2 * twos:2]
    margin = jnp.minimum(donor - 1, most - sink)
    shifted = jax.random.randint(jax.random.fold_in(rng, 1), (twos,), 0, 1 << 20) % (margin + 1)
    sizes = sizes.at[1:1 + 2 * twos:2].set(donor - shifted).at[2:2 + 2 * twos:2].set(sink + shifted)
    return sizes[jax.random.permutation(jax.random.fold_in(rng, 2), amount)]


def bell_draw(own_key, shape, scale, reach, shards=(), held_as=jnp.bfloat16):
    array = jax.random.normal(own_key, shape, jnp.float32) * scale
    if len(shards) > 0:
        array = block_scale(own_key, shape, shards, -0.22, 0.18) * array
    return jnp.clip(array, min=-reach, max=reach).astype(held_as)


def setup_inputs(seed: int = 0) -> dict:
    key_list = jax.random.split(jax.random.key(seed), 13)
    leaf_pattern = bell_draw(key_list[0], (2, NLEAF, KL), 1.0, 6.0, ((1, 128),), jnp.float32)
    leaf_parent = jax.vmap(lambda own: jnp.searchsorted(jnp.cumsum(ragged(own, PAR_DEV, LEAF_DEV, 8, 2)), jnp.arange(LEAF_DEV), side="right"))(jax.random.split(key_list[1], DEVICES)).reshape((DEVICES, LEAF_DEV)).astype(jnp.int32)
    octant = touch_ends(jax.random.randint(key_list[2], (NLEAF,), 0, 8), jax.random.fold_in(key_list[2], 1), 0, 7).astype(jnp.int32)
    interp_theta = bell_draw(key_list[3], (TT, TL), TL ** -0.5, 1.0, (), jnp.float32)
    interp_phi = bell_draw(key_list[4], (PT, PL), PL ** -0.5, 0.75, (), jnp.float32)
    shift_angle = jnp.clip(jax.random.uniform(key_list[5], (8, KT), jnp.float32, -3.140625, 3.140625), -3.140625, 3.140625)
    near_src = draw_near_src(jax.random.fold_in(key_list[12], 71), 0)
    near_type = touch_ends(jax.random.randint(key_list[7], (NLEAF, MN), 0, NTYPE), jax.random.fold_in(key_list[7], 1), 0, NTYPE - 1).astype(jnp.int32)
    leaf_transfer = bell_draw(key_list[8], (2, NTYPE, KL), (2 * MN) ** -0.5, 1.0, (), jnp.float32)
    inter_src = draw_inter_src(jax.random.fold_in(key_list[12], 71), 0)
    inter_type = touch_ends(jax.random.randint(key_list[10], (NT, M), 0, NTYPE), jax.random.fold_in(key_list[10], 1), 0, NTYPE - 1).astype(jnp.int32)
    top_transfer = bell_draw(key_list[11], (2, NTYPE, KT), (8 * M) ** -0.5, 0.375, ((2, 16),), jnp.float32)
    return {"leaf_pattern": leaf_pattern, "leaf_parent": leaf_parent, "octant": octant, "interp_theta": interp_theta, "interp_phi": interp_phi, "shift_angle": shift_angle, "near_src": near_src, "near_type": near_type, "leaf_transfer": leaf_transfer, "inter_src": inter_src, "inter_type": inter_type, "top_transfer": top_transfer}


PRECISE = lax.Precision.HIGHEST


def aggregate(pattern, octs, parent_row, interp_theta, interp_phi, shift_angle, count):
    leaves = pattern.shape[1]
    grid = pattern.reshape(2, leaves, TL, PL)
    section_one = jnp.einsum('cntp,qp->cntq', grid, interp_phi, precision=PRECISE)
    section_two = jnp.matmul(interp_theta, section_one, precision=PRECISE).reshape(2, leaves, TT * PT)
    octant_hot = (octs[:, None] == jnp.arange(8, dtype=jnp.int32)[None, :]).astype(jnp.float32)
    cosine = jnp.dot(octant_hot, jnp.cos(shift_angle), precision=PRECISE)
    sine = jnp.dot(octant_hot, jnp.sin(shift_angle), precision=PRECISE)
    real_part = section_two[0] * cosine - section_two[1] * sine
    imag_part = section_two[0] * sine + section_two[1] * cosine
    parent_hot = (parent_row[None, :] == jnp.arange(count, dtype=jnp.int32)[:, None]).astype(jnp.float32)
    return jnp.stack([jnp.dot(parent_hot, real_part, precision=PRECISE), jnp.dot(parent_hot, imag_part, precision=PRECISE)])


def translate(sources, source_rows, type_rows, table):
    total = source_rows.shape[0]
    samples = sources.shape[2]
    joined = jnp.concatenate([sources[0], sources[1]], axis=1)
    factors = jnp.concatenate([table[0], table[1]], axis=1)
    real_sum = jnp.zeros((total, samples), jnp.float32)
    imag_sum = jnp.zeros((total, samples), jnp.float32)
    for entry in range(source_rows.shape[1]):
        picked = joined[source_rows[:, entry]]
        weights = factors[type_rows[:, entry]]
        src_real = picked[:, :samples]
        src_imag = picked[:, samples:]
        fac_real = weights[:, :samples]
        fac_imag = weights[:, samples:]
        real_sum = real_sum + (fac_real * src_real - fac_imag * src_imag)
        imag_sum = imag_sum + (fac_real * src_imag + fac_imag * src_real)
    return jnp.stack([real_sum, imag_sum])


def reference(leaf_pattern, leaf_parent, octant, interp_theta, interp_phi, shift_angle, near_src, near_type, leaf_transfer, inter_src, inter_type, top_transfer):
    per_device = jnp.transpose(leaf_pattern.reshape(2, DEVICES, LEAF_DEV, KL), (1, 0, 2, 3))
    octs = octant.reshape(DEVICES, LEAF_DEV)

    def one_device(items):
        return aggregate(items[0], items[1], items[2], interp_theta, interp_phi, shift_angle, PAR_DEV)

    parents = lax.map(one_device, (per_device, octs, leaf_parent))
    parents = jnp.transpose(parents, (1, 0, 2, 3)).reshape(2, NT, KT)
    incoming = translate(parents, inter_src, inter_type, top_transfer)
    leaf_incoming = translate(leaf_pattern, near_src, near_type, leaf_transfer)
    return (incoming, leaf_incoming)
```

```python
import jax
import jax.numpy as jnp
from jax import lax
from jax.experimental import pallas as pl
from jax.experimental.pallas import tpu as pltpu
from jax.sharding import PartitionSpec as P

TL = 32
PL = 64
TT = 64
PT = 128
PAR_DEV = 8
REACH = 16
NTYPE = 316
LANES = 128
F32 = jnp.float32
BF16 = jnp.bfloat16


def split(x):
    hi = x.astype(BF16)
    lo = (x - hi.astype(F32)).astype(BF16)
    return hi, lo


def cos_sin(x):
    turns = jnp.round(x * 0.63661977236758134)
    r = (x - turns * 1.5703125) - turns * 4.83826794896619e-4
    z = r * r
    s = r + r * z * (-1.6666654611e-1 + z * (8.3321608736e-3 + z * -1.9515295891e-4))
    c = 1.0 - 0.5 * z + z * z * (4.166664568298827e-2 + z * (-1.388731625493765e-3 + z * 2.443315711809948e-5))
    odd = (turns == 1.0) | (turns == -1.0)
    half = (turns == 2.0) | (turns == -2.0)
    big_c = jnp.where(odd, s, c)
    big_s = jnp.where(odd, c, s)
    cosine = jnp.where(half | (turns == 1.0), -big_c, big_c)
    sine = jnp.where(half | (turns == -1.0), -big_s, big_s)
    return cosine, sine


def aggregate_kernel(oct_ref, par_ref, x_ref, theta_ref, phi_ref, angle_ref, out_ref, y_ref, ct_ref, st_ref, acc_ref, th_ref):
    leaves = x_ref.shape[1]
    dirs = out_ref.shape[0]
    rows = 8 * dirs
    for k in range(TT):
        cosine, sine = cos_sin(angle_ref[:, k * LANES:(k + 1) * LANES])
        row = (k // 4) * 8 + k % 4
        ct_ref[pl.ds(row, 8, stride=rows), :] = cosine
        ct_ref[pl.ds(row + 4, 8, stride=rows), :] = cosine
        st_ref[pl.ds(row, 8, stride=rows), :] = sine
        st_ref[pl.ds(row + 4, 8, stride=rows), :] = -sine
    th_ref[...] = jnp.zeros_like(th_ref)
    for d in range(dirs):
        th_ref[8 * d:8 * d + 4, 0:TL] = theta_ref[4 * d:4 * d + 4, :]
        th_ref[8 * d + 4:8 * d + 8, TL:2 * TL] = theta_ref[4 * d:4 * d + 4, :]
    th_hi, th_lo = split(th_ref[...])
    th = jnp.concatenate([th_hi, th_hi, th_lo], axis=1)
    phi = phi_ref[...]
    zero = jnp.zeros_like(phi)
    pair = jnp.concatenate([jnp.concatenate([phi, zero], axis=1), jnp.concatenate([zero, phi], axis=1)], axis=0)
    ph_hi, ph_lo = split(pair)
    dims = (((1,), (1,)), ((), ()))
    for u in range(TL // 2):
        block = jnp.concatenate([x_ref[0, :, u * LANES:(u + 1) * LANES], x_ref[1, :, u * LANES:(u + 1) * LANES]], axis=0)
        hi, lo = split(block)
        y = (
            lax.dot_general(hi, ph_hi, dims, preferred_element_type=F32)
            + lax.dot_general(lo, ph_hi, dims, preferred_element_type=F32)
            + lax.dot_general(hi, ph_lo, dims, preferred_element_type=F32)
        )
        y_ref[4 * u * leaves:(4 * u + 2) * leaves, :] = y[:, :LANES]
        y_ref[(4 * u + 2) * leaves:(4 * u + 4) * leaves, :] = y[:, LANES:]
    acc_ref[...] = jnp.zeros_like(acc_ref)
    step = 2 * leaves

    def polar(n):
        parts = [
            y_ref[pl.ds(c * leaves + n + t0 * step, 8, stride=step), :]
            for c in range(2)
            for t0 in range(0, TL, 8)
        ]
        return jnp.concatenate(parts, axis=0)

    def body(m, carry):
        y = jnp.concatenate([polar(2 * m), polar(2 * m + 1)], axis=1)
        hi, lo = split(y)
        f = jnp.dot(th, jnp.concatenate([hi, lo, hi], axis=0), preferred_element_type=F32)
        for k in range(2):
            n = 2 * m + k
            tab = pl.multiple_of(oct_ref[n] * rows, rows)
            par = pl.multiple_of(par_ref[0, n] * (2 * rows), 2 * rows)
            fk = f[:, k * LANES:(k + 1) * LANES]
            acc_ref[pl.ds(par, rows), :] += fk * ct_ref[pl.ds(tab, rows), :]
            acc_ref[pl.ds(par + rows, rows), :] += fk * st_ref[pl.ds(tab, rows), :]
        return carry

    lax.fori_loop(0, leaves // 2, body, 0)
    for p in range(PAR_DEV):
        for d in range(dirs):
            a = acc_ref[p * 2 * rows + 8 * d:p * 2 * rows + 8 * d + 8, :]
            b = acc_ref[p * 2 * rows + rows + 8 * d:p * 2 * rows + rows + 8 * d + 8, :]
            out_ref[d, 8 * p:8 * p + 8, :] = a + pltpu.roll(b, 4, 0)


def aggregate(pattern, octs, parents, theta, phi, angle, dirs):
    leaves = pattern.shape[1]
    vmem = pl.BlockSpec(memory_space=pltpu.VMEM)
    smem = pl.BlockSpec(memory_space=pltpu.SMEM)
    return pl.pallas_call(
        aggregate_kernel,
        out_shape=jax.ShapeDtypeStruct((dirs, PAR_DEV * 8, LANES), F32),
        in_specs=[smem, smem, vmem, vmem, vmem, vmem],
        out_specs=vmem,
        scratch_shapes=[
            pltpu.VMEM((TL * 2 * leaves, LANES), F32),
            pltpu.VMEM((8 * 8 * dirs, LANES), F32),
            pltpu.VMEM((8 * 8 * dirs, LANES), F32),
            pltpu.VMEM((PAR_DEV * 2 * 8 * dirs, LANES), F32),
            pltpu.VMEM((8 * dirs, 2 * TL), F32),
        ],
        compiler_params=pltpu.CompilerParams(vmem_limit_bytes=16 * 1024 * 1024),
        cost_estimate=pl.CostEstimate(flops=600_000_000, bytes_accessed=2_000_000, transcendentals=0),
        name="aggregate",
    )(octs, parents, pattern, theta, phi, angle)


def top_kernel(src_ref, type_ref, own_ref, low_ref, high_ref, table_ref, out_ref, box_ref, tab_ref, sum_ref):
    boxes = own_ref.shape[0] // 8
    types = table_ref.shape[1]
    span = 8 * boxes
    box_ref[0:span, :] = low_ref[...]
    box_ref[span:2 * span, :] = own_ref[...]
    box_ref[2 * span:3 * span, :] = high_ref[...]
    for first in range(0, types, 8):
        count = min(8, types - first)
        for c in range(4):
            real = table_ref[0, first:first + count, c * LANES:(c + 1) * LANES]
            imag = table_ref[1, first:first + count, c * LANES:(c + 1) * LANES]
            row = first * 16 + c
            tab_ref[pl.ds(row, count, stride=16), :] = real
            tab_ref[pl.ds(row + 4, count, stride=16), :] = real
            tab_ref[pl.ds(row + 8, count, stride=16), :] = imag
            tab_ref[pl.ds(row + 12, count, stride=16), :] = -imag

    def body(r, carry):
        one = [jnp.zeros((8, LANES), F32)] * 2
        two = [jnp.zeros((8, LANES), F32)] * 2
        for j in range(src_ref.shape[1]):
            s = pl.multiple_of(src_ref[r, j], 8)
            t = pl.multiple_of(type_ref[r, j], 16)
            a = box_ref[pl.ds(s, 8), :]
            one[j % 2] = one[j % 2] + a * tab_ref[pl.ds(t, 8), :]
            two[j % 2] = two[j % 2] + a * tab_ref[pl.ds(t + 8, 8), :]
        sum_ref[pl.ds(pl.multiple_of(8 * r, 8), 8), :] = (one[0] + one[1]) + pltpu.roll(two[0] + two[1], 4, 0)
        return carry

    lax.fori_loop(0, boxes, body, 0)
    for r in range(0, boxes, 8):
        for part in range(2):
            for c in range(4):
                out_ref[part, r:r + 8, c * LANES:(c + 1) * LANES] = sum_ref[pl.ds(8 * r + 4 * part + c, 8, stride=8), :]


def top_translate(src, kind, own, low, high, table):
    boxes = src.shape[0]
    vmem = pl.BlockSpec(memory_space=pltpu.VMEM)
    smem = pl.BlockSpec(memory_space=pltpu.SMEM)
    return pl.pallas_call(
        top_kernel,
        out_shape=jax.ShapeDtypeStruct((2, boxes, table.shape[2]), F32),
        in_specs=[smem, smem, vmem, vmem, vmem, vmem],
        out_specs=vmem,
        scratch_shapes=[
            pltpu.VMEM((3 * 8 * boxes, LANES), F32),
            pltpu.VMEM((table.shape[1] * 16, LANES), F32),
            pltpu.VMEM((8 * boxes, LANES), F32),
        ],
        compiler_params=pltpu.CompilerParams(vmem_limit_bytes=16 * 1024 * 1024),
        cost_estimate=pl.CostEstimate(flops=16_000_000, bytes_accessed=16_000_000, transcendentals=0),
        name="top_translate",
    )(src, kind, own, low, high, table)


def leaf_kernel(src_ref, type_ref, own_ref, low_ref, high_ref, table_ref, out_ref, leaf_ref, tab_ref, sum_ref):
    leaves = own_ref.shape[1]
    reach = low_ref.shape[1]
    types = table_ref.shape[1]
    chunks = own_ref.shape[2] // LANES
    size = 2 * chunks
    for ref, start in ((low_ref, 0), (own_ref, reach), (high_ref, reach + leaves)):
        for first in range(0, ref.shape[1], 8):
            for part in range(2):
                for c in range(chunks):
                    leaf_ref[pl.ds((start + first) * size + part * chunks + c, 8, stride=size), :] = ref[
                        part, first:first + 8, c * LANES:(c + 1) * LANES
                    ]
    for first in range(0, types, 8):
        count = min(8, types - first)
        for part in range(2):
            for c in range(chunks):
                tab_ref[pl.ds(first * size + part * chunks + c, count, stride=size), :] = table_ref[
                    part, first:first + count, c * LANES:(c + 1) * LANES
                ]

    def body(i, carry):
        real = jnp.zeros((chunks, LANES), F32)
        imag = jnp.zeros((chunks, LANES), F32)
        for j in range(src_ref.shape[1]):
            s = pl.multiple_of(src_ref[i, j], size)
            t = pl.multiple_of(type_ref[i, j], size)
            sr = leaf_ref[pl.ds(s, chunks), :]
            si = leaf_ref[pl.ds(s + chunks, chunks), :]
            fr = tab_ref[pl.ds(t, chunks), :]
            fi = tab_ref[pl.ds(t + chunks, chunks), :]
            real = real + (fr * sr - fi * si)
            imag = imag + (fr * si + fi * sr)
        at = pl.multiple_of(i * size, size)
        sum_ref[pl.ds(at, chunks), :] = real
        sum_ref[pl.ds(at + chunks, chunks), :] = imag
        return carry

    lax.fori_loop(0, leaves, body, 0)
    for first in range(0, leaves, 8):
        for part in range(2):
            for c in range(chunks):
                out_ref[part, first:first + 8, c * LANES:(c + 1) * LANES] = sum_ref[
                    pl.ds(first * size + part * chunks + c, 8, stride=size), :
                ]


def leaf_translate(src, kind, own, low, high, table):
    leaves = own.shape[1]
    reach = low.shape[1]
    size = 2 * own.shape[2] // LANES
    vmem = pl.BlockSpec(memory_space=pltpu.VMEM)
    smem = pl.BlockSpec(memory_space=pltpu.SMEM)
    return pl.pallas_call(
        leaf_kernel,
        out_shape=jax.ShapeDtypeStruct(own.shape, F32),
        in_specs=[smem, smem, vmem, vmem, vmem, vmem],
        out_specs=vmem,
        scratch_shapes=[
            pltpu.VMEM(((leaves + 2 * reach) * size, LANES), F32),
            pltpu.VMEM((table.shape[1] * size, LANES), F32),
            pltpu.VMEM((leaves * size, LANES), F32),
        ],
        compiler_params=pltpu.CompilerParams(vmem_limit_bytes=32 * 1024 * 1024),
        cost_estimate=pl.CostEstimate(flops=12_000_000, bytes_accessed=12_000_000, transcendentals=0),
        name="leaf_translate",
    )(src, kind, own, low, high, table)


def shifts(axis):
    count = lax.axis_size(axis)
    forward = [(i, i + 1) for i in range(count - 1)]
    return forward, [(b, a) for a, b in forward]


def per_device(
    leaf_pattern,
    leaf_parent,
    octant,
    interp_theta,
    interp_phi,
    shift_angle,
    near_src,
    near_type,
    leaf_transfer,
    inter_src,
    inter_type,
    top_transfer,
):
    leaves = leaf_pattern.shape[1]
    dirs = lax.axis_size("dir")
    up, down = shifts(("box", "dir"))
    leaf_low = lax.ppermute(leaf_pattern[:, leaves - REACH:], ("box", "dir"), up)
    leaf_high = lax.ppermute(leaf_pattern[:, :REACH], ("box", "dir"), down)

    parents = aggregate(leaf_pattern, octant, leaf_parent, interp_theta, interp_phi, shift_angle, dirs)
    directed = lax.all_to_all(parents, "dir", split_axis=0, concat_axis=0)
    own = directed.reshape(-1, LANES)
    boxes = inter_src.shape[0]
    up, down = shifts("box")
    low = lax.ppermute(own, "box", up)
    high = lax.ppermute(own, "box", down)
    top_src = (inter_src - (lax.axis_index("box") - 1) * boxes) * 8
    incoming = top_translate(top_src, inter_type * 16, own, low, high, top_transfer)

    size = 2 * leaf_pattern.shape[2] // LANES
    first_leaf = lax.axis_index(("box", "dir")) * leaves
    leaf_src = (near_src - (first_leaf - REACH)) * size
    leaf_incoming = leaf_translate(leaf_src, near_type * size, leaf_pattern, leaf_low, leaf_high, leaf_transfer)
    return (incoming, leaf_incoming)


def solution(mesh):
    return jax.shard_map(
        per_device,
        mesh=mesh,
        in_specs=(
            P(None, ("box", "dir"), None),
            P(("box", "dir"), None),
            P(("box", "dir")),
            P(),
            P(),
            P(),
            P(("box", "dir"), None),
            P(("box", "dir"), None),
            P(),
            P("box", None),
            P("box", None),
            P(None, None, "dir"),
        ),
        out_specs=(P(None, "box", "dir"), P(None, ("box", "dir"), None)),
        check_vma=False,
    )
```

```python
import jax
import jax.numpy as jnp
from jax import lax
from jax.experimental import pallas as pl
from jax.experimental.pallas import tpu as pltpu
from jax.sharding import PartitionSpec as P

TL = 32
PL = 64
TT = 64
PT = 128
PAR_DEV = 8
REACH = 16
LANES = 128
PAD = 8
F32 = jnp.float32
BF16 = jnp.bfloat16
I32 = jnp.int32
MIB = 1024 * 1024
VMEM = pl.BlockSpec(memory_space=pltpu.VMEM)
SMEM = pl.BlockSpec(memory_space=pltpu.SMEM)
HBM = pl.BlockSpec(memory_space=pltpu.HBM)


def split(x):
    hi = x.astype(BF16)
    lo = (x - hi.astype(F32)).astype(BF16)
    return hi, lo


def cos_sin(x):
    turns = jnp.round(x * 0.63661977236758134)
    r = (x - turns * 1.5703125) - turns * 4.83826794896619e-4
    z = r * r
    s = r + r * z * (-1.6666654611e-1 + z * (8.3321608736e-3 + z * -1.9515295891e-4))
    c = 1.0 - 0.5 * z + z * z * (4.166664568298827e-2 + z * (-1.388731625493765e-3 + z * 2.443315711809948e-5))
    size = jnp.abs(turns)
    odd = size == 1.0
    half = size == 2.0
    big_c = jnp.where(odd, s, c)
    big_s = jnp.where(odd, c, s)
    cosine = jnp.where(half | (turns == 1.0), -big_c, big_c)
    sine = jnp.where(half | (turns == -1.0), -big_s, big_s)
    return cosine, sine


def exchange(x):
    even = lax.broadcasted_iota(I32, x.shape, 0) % 2 == 0
    return jnp.where(even, pltpu.roll(x, x.shape[0] - 1, 0), pltpu.roll(x, 1, 0))


def estimate(microseconds):
    return pl.CostEstimate(flops=1000, bytes_accessed=int(microseconds * 3_000_000), transcendentals=0)


def aggregate_kernel(
    oct_hbm,
    par_hbm,
    x_hbm,
    theta_hbm,
    phi_hbm,
    angle_hbm,
    out_ref,
    low_hbm,
    high_hbm,
    oct_ref,
    par_ref,
    x_ref,
    theta_ref,
    phi_ref,
    angle_ref,
    y_ref,
    ct_ref,
    st_ref,
    sem,
):
    leaves = x_ref.shape[1]
    rows = 2 * TT
    pitch = rows + PAD
    line = TL + PAD
    reach = low_hbm.shape[1]
    gets = [
        pltpu.make_async_copy(source, target, sem.at[i])
        for i, (source, target) in enumerate(
            (
                (angle_hbm, angle_ref),
                (theta_hbm, theta_ref),
                (phi_hbm, phi_ref),
                (x_hbm, x_ref),
                (oct_hbm, oct_ref),
                (par_hbm, par_ref),
            )
        )
    ]
    puts = [
        pltpu.make_async_copy(x_hbm.at[:, 0:reach, :], low_hbm, sem.at[6]),
        pltpu.make_async_copy(x_hbm.at[:, leaves - reach:leaves, :], high_hbm, sem.at[7]),
    ]
    for get in gets:
        get.start()
    for put in puts:
        put.start()
    get_angle, get_theta, get_phi, get_x, get_oct, get_par = gets
    out_ref[...] = jnp.zeros_like(out_ref)
    get_angle.wait()
    for s in range(TT):
        cosine, sine = cos_sin(angle_ref[:, s * LANES:(s + 1) * LANES])
        ct_ref[pl.ds(2 * s, 8, stride=pitch), :] = cosine
        ct_ref[pl.ds(2 * s + 1, 8, stride=pitch), :] = cosine
        st_ref[pl.ds(2 * s, 8, stride=pitch), :] = -sine
        st_ref[pl.ds(2 * s + 1, 8, stride=pitch), :] = sine
    get_theta.wait()
    hi, lo = split(theta_ref[...])
    stack = jnp.concatenate([hi, hi, hi, hi, lo, lo], axis=0)
    row = lax.broadcasted_iota(jnp.int32, (rows, TT), 0)
    col = lax.broadcasted_iota(jnp.int32, (rows, TT), 1)
    pick = jnp.where(row // 2 == col, 1.0, 0.0).astype(BF16)
    dims = (((1,), (1,)), ((), ()))
    wide = lax.dot_general(pick, stack, dims, preferred_element_type=F32)
    row = lax.broadcasted_iota(jnp.int32, wide.shape, 0)
    col = lax.broadcasted_iota(jnp.int32, wide.shape, 1)
    same = row % 2 == (col // TL) % 2
    th = jnp.concatenate([jnp.where(same, wide, 0.0), jnp.where(same, 0.0, wide)], axis=0).astype(BF16)
    get_phi.wait()
    phi = phi_ref[...]
    zero = jnp.zeros_like(phi)
    pair = jnp.concatenate([jnp.concatenate([phi, zero], axis=1), jnp.concatenate([zero, phi], axis=1)], axis=0)
    ph_hi, ph_lo = split(pair)
    ph_two = jnp.concatenate([ph_hi, ph_hi], axis=0)
    get_x.wait()
    for u in range(TL // 2):
        lanes = slice(u * LANES, (u + 1) * LANES)
        block = jnp.concatenate([x_ref[0, :, lanes], x_ref[1, :, lanes]], axis=0)
        hi, lo = split(block)
        y = jnp.dot(jnp.concatenate([hi, lo], axis=1), ph_two, preferred_element_type=F32) + jnp.dot(
            hi, ph_lo, preferred_element_type=F32
        )
        for g in range(0, 2 * leaves, 8):
            y_ref[pl.ds(g * line + 2 * u, 8, stride=line), :] = y[g:g + 8, :LANES]
            y_ref[pl.ds(g * line + 2 * u + 1, 8, stride=line), :] = y[g:g + 8, LANES:]

    def polar(n):
        return jnp.concatenate(
            [
                y_ref[pl.ds(pl.multiple_of(n * line, 8), TL), :],
                y_ref[pl.ds(pl.multiple_of((leaves + n) * line, 8), TL), :],
            ],
            axis=0,
        )

    get_oct.wait()
    get_par.wait()

    def body(m, carry):
        y = jnp.concatenate([polar(2 * m), polar(2 * m + 1)], axis=1)
        hi, lo = split(y)
        f = jnp.dot(th, jnp.concatenate([hi, lo, hi], axis=0), preferred_element_type=F32)
        for k in range(2):
            n = 2 * m + k
            tab = pl.multiple_of(oct_ref[n] * pitch, 8)
            par = pl.multiple_of(par_ref[0, n] * 8, 8)
            lanes = slice(k * LANES, (k + 1) * LANES)
            values = [
                f[8 * d:8 * d + 8, lanes] * ct_ref[pl.ds(tab + 8 * d, 8), :]
                + f[rows + 8 * d:rows + 8 * d + 8, lanes] * st_ref[pl.ds(tab + 8 * d, 8), :]
                for d in range(rows // 8)
            ]
            values = [value + out_ref[d, pl.ds(par, 8), :] for d, value in enumerate(values)]
            for d, value in enumerate(values):
                out_ref[d, pl.ds(par, 8), :] = value
        return carry

    lax.fori_loop(0, leaves // 2, body, 0, unroll=8)
    for put in puts:
        put.wait()


def aggregate(pattern, octs, parents, theta, phi, angle, dirs):
    leaves = pattern.shape[1]
    edge = jax.ShapeDtypeStruct((2, REACH, pattern.shape[2]), F32)
    return pl.pallas_call(
        aggregate_kernel,
        out_shape=(jax.ShapeDtypeStruct((dirs, PAR_DEV * 8, LANES), F32), edge, edge),
        in_specs=[HBM] * 6,
        out_specs=(VMEM, HBM, HBM),
        scratch_shapes=[
            pltpu.SMEM(octs.shape, I32),
            pltpu.SMEM(parents.shape, I32),
            pltpu.VMEM(pattern.shape, F32),
            pltpu.VMEM(theta.shape, F32),
            pltpu.VMEM(phi.shape, F32),
            pltpu.VMEM(angle.shape, F32),
            pltpu.VMEM(((TL + PAD) * 2 * leaves, LANES), F32),
            pltpu.VMEM((8 * (2 * TT + PAD), LANES), F32),
            pltpu.VMEM((8 * (2 * TT + PAD), LANES), F32),
            pltpu.SemaphoreType.DMA((8,)),
        ],
        compiler_params=pltpu.CompilerParams(vmem_limit_bytes=60 * MIB),
        cost_estimate=estimate(5),
        name="aggregate",
    )(octs, parents, pattern, theta, phi, angle)


def prepare_kernel(table_ref, after_hbm, out_ref):
    for t in range(table_ref.shape[0] // 8):
        tile = table_ref[8 * t:8 * t + 8, :]
        out_ref[16 * t:16 * t + 8, :] = tile
        out_ref[16 * t + 8:16 * t + 16, :] = exchange(tile)


def prepare(table, after):
    return pl.pallas_call(
        prepare_kernel,
        out_shape=jax.ShapeDtypeStruct((2 * table.shape[0], LANES), F32),
        in_specs=[VMEM, HBM],
        out_specs=VMEM,
        compiler_params=pltpu.CompilerParams(vmem_limit_bytes=12 * MIB),
        cost_estimate=estimate(1.5),
        name="prepare",
    )(table, after)


def top_kernel(src_ref, type_ref, own_ref, mate_ref, cross_ref, tab_ref, out_ref, box_ref, one_ref, two_ref):
    boxes = own_ref.shape[0] // 8
    entries = src_ref.shape[0] // boxes
    span = 8 * boxes
    box_ref[0:span, :] = own_ref[...]
    box_ref[span:2 * span, :] = mate_ref[...]
    box_ref[2 * span:3 * span, :] = cross_ref[...]

    def body(r, carry):
        one = [jnp.zeros((8, LANES), F32)] * 2
        two = [jnp.zeros((8, LANES), F32)] * 2
        for j in range(entries):
            s = pl.multiple_of(src_ref[j * boxes + r], 8)
            t = pl.multiple_of(type_ref[j * boxes + r], 16)
            a = box_ref[pl.ds(s, 8), :]
            one[j % 2] = one[j % 2] + a * tab_ref[pl.ds(t, 8), :]
            two[j % 2] = two[j % 2] + a * tab_ref[pl.ds(t + 8, 8), :]
        at = pl.ds(pl.multiple_of(8 * r, 8), 8)
        one_ref[at, :] = one[0] + one[1]
        two_ref[at, :] = two[0] + two[1]
        return carry

    lax.fori_loop(0, boxes, body, 0)
    for r in range(0, boxes, 8):
        for c in range(4):
            lanes = slice(c * LANES, (c + 1) * LANES)
            even = pl.ds(8 * r + 2 * c, 8, stride=8)
            odd = pl.ds(8 * r + 2 * c + 1, 8, stride=8)
            out_ref[0, r:r + 8, lanes] = one_ref[even, :] - one_ref[odd, :]
            out_ref[1, r:r + 8, lanes] = two_ref[even, :] + two_ref[odd, :]


def top_translate(src, kind, own, mate, cross, table):
    rows = own.shape[0]
    return pl.pallas_call(
        top_kernel,
        out_shape=jax.ShapeDtypeStruct((2, rows // 8, 4 * LANES), F32),
        in_specs=[SMEM, SMEM, VMEM, VMEM, VMEM, VMEM],
        out_specs=VMEM,
        scratch_shapes=[
            pltpu.VMEM((3 * rows, LANES), F32),
            pltpu.VMEM((rows, LANES), F32),
            pltpu.VMEM((rows, LANES), F32),
        ],
        compiler_params=pltpu.CompilerParams(vmem_limit_bytes=12 * MIB),
        cost_estimate=estimate(9),
        name="top_translate",
    )(src, kind, own, mate, cross, table)


def leaf_kernel(src_ref, type_ref, own_hbm, low_hbm, high_hbm, table_hbm, after_hbm, out_ref, own_ref, low_ref, high_ref, tab_ref, leaf_ref, one_ref, two_ref, sem):
    leaves = own_ref.shape[1]
    reach = low_ref.shape[1]
    chunks = own_ref.shape[2] // LANES
    size = 2 * chunks
    pitch = 2 * size + PAD
    gets = [
        pltpu.make_async_copy(source, target, sem.at[i])
        for i, (source, target) in enumerate(
            ((own_hbm, own_ref), (low_hbm, low_ref), (high_hbm, high_ref), (table_hbm, tab_ref))
        )
    ]
    for get in gets:
        get.start()
    for get in gets[:3]:
        get.wait()
    for ref, start in ((low_ref, 0), (own_ref, reach), (high_ref, reach + leaves)):
        for first in range(0, ref.shape[1], 8):
            for c in range(chunks):
                lanes = slice(c * LANES, (c + 1) * LANES)
                real = ref[0, first:first + 8, lanes]
                imag = ref[1, first:first + 8, lanes]
                at = (start + first) * pitch + 2 * c
                leaf_ref[pl.ds(at, 8, stride=pitch), :] = real
                leaf_ref[pl.ds(at + 1, 8, stride=pitch), :] = imag
                leaf_ref[pl.ds(at + size, 8, stride=pitch), :] = imag
                leaf_ref[pl.ds(at + size + 1, 8, stride=pitch), :] = real
    gets[3].wait()
    line = size + PAD

    def body(i, carry):
        one = jnp.zeros((size, LANES), F32)
        two = jnp.zeros((size, LANES), F32)
        for j in range(src_ref.shape[0]):
            s = pl.multiple_of(src_ref[j, i], 8)
            t = pl.multiple_of(type_ref[j, i], size)
            tab = tab_ref[pl.ds(t, size), :]
            one = one + tab * leaf_ref[pl.ds(s, size), :]
            two = two + tab * leaf_ref[pl.ds(s + size, size), :]
        at = pl.ds(pl.multiple_of(i * line, 8), size)
        one_ref[at, :] = one
        two_ref[at, :] = two
        return carry

    lax.fori_loop(0, leaves, body, 0)
    for first in range(0, leaves, 8):
        for c in range(chunks):
            lanes = slice(c * LANES, (c + 1) * LANES)
            even = pl.ds(first * line + 2 * c, 8, stride=line)
            odd = pl.ds(first * line + 2 * c + 1, 8, stride=line)
            out_ref[0, first:first + 8, lanes] = one_ref[even, :] - one_ref[odd, :]
            out_ref[1, first:first + 8, lanes] = two_ref[even, :] + two_ref[odd, :]


def leaf_translate(src, kind, own, low, high, table, after):
    leaves = own.shape[1]
    reach = low.shape[1]
    size = 2 * own.shape[2] // LANES
    line = size + PAD
    return pl.pallas_call(
        leaf_kernel,
        out_shape=jax.ShapeDtypeStruct(own.shape, F32),
        in_specs=[SMEM, SMEM, HBM, HBM, HBM, HBM, HBM],
        out_specs=VMEM,
        scratch_shapes=[
            pltpu.VMEM(own.shape, F32),
            pltpu.VMEM(low.shape, F32),
            pltpu.VMEM(high.shape, F32),
            pltpu.VMEM(table.shape, F32),
            pltpu.VMEM(((leaves + 2 * reach) * (2 * size + PAD), LANES), F32),
            pltpu.VMEM((leaves * line, LANES), F32),
            pltpu.VMEM((leaves * line, LANES), F32),
            pltpu.SemaphoreType.DMA((4,)),
        ],
        compiler_params=pltpu.CompilerParams(vmem_limit_bytes=40 * MIB),
        cost_estimate=estimate(5),
        name="leaf_translate",
    )(src, kind, own, low, high, table, after)


def interleaved(table):
    types = table.shape[1]
    view = table.reshape(2, types, -1, LANES)
    return view.transpose(1, 2, 0, 3).reshape(-1, LANES)


def per_device(
    leaf_pattern,
    leaf_parent,
    octant,
    interp_theta,
    interp_phi,
    shift_angle,
    near_src,
    near_type,
    leaf_transfer,
    inter_src,
    inter_type,
    top_transfer,
):
    leaves = leaf_pattern.shape[1]
    dirs = lax.axis_size("dir")
    groups = lax.axis_size("box")
    box = lax.axis_index("box")
    parents, low, high = aggregate(
        leaf_pattern, octant, leaf_parent, interp_theta.T, interp_phi.T, shift_angle, dirs
    )
    directed = lax.all_to_all(parents, "dir", split_axis=0, concat_axis=0)
    count = dirs * groups
    leaf_low = lax.ppermute(high, ("box", "dir"), [(i, i + 1) for i in range(count - 1)])
    leaf_high = lax.ppermute(low, ("box", "dir"), [(i + 1, i) for i in range(count - 1)])

    own = directed.reshape(-1, LANES)
    boxes = inter_src.shape[0]
    mate = lax.ppermute(own, "box", [(i, i ^ 1) for i in range(groups)])
    cross = lax.ppermute(own, "box", [(i, ((i + 1) ^ 1) - 1) for i in range(1, groups - 1)])
    table = prepare(interleaved(top_transfer), low)
    src = inter_src.T
    group = src // boxes
    place = jnp.where(group == box, 0, jnp.where(group == (box ^ 1), boxes, 2 * boxes)) + src % boxes
    top_src = (place * 8).reshape(-1)
    top_type = (inter_type.T * 16).reshape(-1)
    incoming = top_translate(top_src, top_type, own, mate, cross, table)

    size = 2 * leaf_pattern.shape[2] // LANES
    first_leaf = lax.axis_index(("box", "dir")) * leaves
    leaf_src = (near_src.T - (first_leaf - REACH)) * (2 * size + PAD)
    leaf_incoming = leaf_translate(
        leaf_src, near_type.T * size, leaf_pattern, leaf_low, leaf_high, interleaved(leaf_transfer), directed
    )
    return (incoming, leaf_incoming)


def solution(mesh):
    return jax.shard_map(
        per_device,
        mesh=mesh,
        in_specs=(
            P(None, ("box", "dir"), None),
            P(("box", "dir"), None),
            P(("box", "dir")),
            P(),
            P(),
            P(),
            P(("box", "dir"), None),
            P(("box", "dir"), None),
            P(),
            P("box", None),
            P("box", None),
            P(None, None, "dir"),
        ),
        out_specs=(P(None, "box", "dir"), P(None, ("box", "dir"), None)),
        check_vma=False,
    )
```

```python
import jax
import jax.numpy as jnp
from jax import lax
from jax.experimental import pallas as pl
from jax.experimental.pallas import tpu as pltpu
from jax.sharding import PartitionSpec as P

TL = 32
PL = 64
TT = 64
PT = 128
PAR_DEV = 8
REACH = 16
LANES = 128
PAD = 8
F32 = jnp.float32
BF16 = jnp.bfloat16
I32 = jnp.int32
MIB = 1024 * 1024
VMEM = pl.BlockSpec(memory_space=pltpu.VMEM)
SMEM = pl.BlockSpec(memory_space=pltpu.SMEM)
HBM = pl.BlockSpec(memory_space=pltpu.HBM)


def split(x):
    hi = x.astype(BF16)
    lo = (x - hi.astype(F32)).astype(BF16)
    return hi, lo


def cos_sin(x):
    turns = jnp.round(x * 0.63661977236758134)
    r = (x - turns * 1.5703125) - turns * 4.83826794896619e-4
    z = r * r
    s = r + r * z * (-1.6666654611e-1 + z * (8.3321608736e-3 + z * -1.9515295891e-4))
    c = 1.0 - 0.5 * z + z * z * (4.166664568298827e-2 + z * (-1.388731625493765e-3 + z * 2.443315711809948e-5))
    size = jnp.abs(turns)
    odd = size == 1.0
    half = size == 2.0
    big_c = jnp.where(odd, s, c)
    big_s = jnp.where(odd, c, s)
    cosine = jnp.where(half | (turns == 1.0), -big_c, big_c)
    sine = jnp.where(half | (turns == -1.0), -big_s, big_s)
    return cosine, sine


def exchange(x):
    even = lax.broadcasted_iota(I32, x.shape, 0) % 2 == 0
    return jnp.where(even, pltpu.roll(x, x.shape[0] - 1, 0), pltpu.roll(x, 1, 0))


def estimate(microseconds):
    return pl.CostEstimate(flops=1000, bytes_accessed=int(microseconds * 3_000_000), transcendentals=0)


def aggregate_kernel(
    oct_hbm,
    par_hbm,
    x_hbm,
    theta_hbm,
    phi_hbm,
    angle_hbm,
    out_ref,
    edge_b_hbm,
    edge_a_hbm,
    oct_ref,
    par_ref,
    x_ref,
    theta_ref,
    phi_ref,
    angle_ref,
    y_ref,
    ct_ref,
    st_ref,
    sem,
):
    leaves = x_ref.shape[1]
    rows = 2 * TT
    pitch = rows + PAD
    line = TL + PAD
    reach = edge_b_hbm.shape[1]
    gets = [
        pltpu.make_async_copy(source, target, sem.at[i])
        for i, (source, target) in enumerate(
            (
                (angle_hbm, angle_ref),
                (theta_hbm, theta_ref),
                (phi_hbm, phi_ref),
                (x_hbm, x_ref),
                (oct_hbm, oct_ref),
                (par_hbm, par_ref),
            )
        )
    ]
    last = leaves - reach
    start_a = pl.multiple_of(jnp.where(lax.axis_index("dir") % 2 == 0, last, 0), 8)
    start_b = pl.multiple_of(last - start_a, 8)
    puts = [
        pltpu.make_async_copy(x_ref.at[:, pl.ds(start_b, reach), :], edge_b_hbm, sem.at[6]),
        pltpu.make_async_copy(x_ref.at[:, pl.ds(start_a, reach), :], edge_a_hbm, sem.at[7]),
    ]
    for get in gets:
        get.start()
    get_angle, get_theta, get_phi, get_x, get_oct, get_par = gets
    out_ref[...] = jnp.zeros_like(out_ref)
    get_angle.wait()
    for s in range(TT):
        cosine, sine = cos_sin(angle_ref[:, s * LANES:(s + 1) * LANES])
        ct_ref[pl.ds(2 * s, 8, stride=pitch), :] = cosine
        ct_ref[pl.ds(2 * s + 1, 8, stride=pitch), :] = cosine
        st_ref[pl.ds(2 * s, 8, stride=pitch), :] = -sine
        st_ref[pl.ds(2 * s + 1, 8, stride=pitch), :] = sine
    get_theta.wait()
    hi, lo = split(theta_ref[...])
    stack = jnp.concatenate([hi, hi, hi, hi, lo, lo], axis=0)
    row = lax.broadcasted_iota(jnp.int32, (rows, TT), 0)
    col = lax.broadcasted_iota(jnp.int32, (rows, TT), 1)
    pick = jnp.where(row // 2 == col, 1.0, 0.0).astype(BF16)
    dims = (((1,), (1,)), ((), ()))
    wide = lax.dot_general(pick, stack, dims, preferred_element_type=F32)
    row = lax.broadcasted_iota(jnp.int32, wide.shape, 0)
    col = lax.broadcasted_iota(jnp.int32, wide.shape, 1)
    same = row % 2 == (col // TL) % 2
    th = jnp.concatenate([jnp.where(same, wide, 0.0), jnp.where(same, 0.0, wide)], axis=0).astype(BF16)
    get_phi.wait()
    phi = phi_ref[...]
    zero = jnp.zeros_like(phi)
    pair = jnp.concatenate([jnp.concatenate([phi, zero], axis=1), jnp.concatenate([zero, phi], axis=1)], axis=0)
    ph_hi, ph_lo = split(pair)
    ph_two = jnp.concatenate([ph_hi, ph_hi], axis=0)
    get_x.wait()
    for put in puts:
        put.start()
    for u in range(TL // 2):
        lanes = slice(u * LANES, (u + 1) * LANES)
        block = jnp.concatenate([x_ref[0, :, lanes], x_ref[1, :, lanes]], axis=0)
        hi, lo = split(block)
        y = jnp.dot(jnp.concatenate([hi, lo], axis=1), ph_two, preferred_element_type=F32) + jnp.dot(
            hi, ph_lo, preferred_element_type=F32
        )
        for g in range(0, 2 * leaves, 8):
            y_ref[pl.ds(g * line + 2 * u, 8, stride=line), :] = y[g:g + 8, :LANES]
            y_ref[pl.ds(g * line + 2 * u + 1, 8, stride=line), :] = y[g:g + 8, LANES:]

    def polar(n):
        return jnp.concatenate(
            [
                y_ref[pl.ds(pl.multiple_of(n * line, 8), TL), :],
                y_ref[pl.ds(pl.multiple_of((leaves + n) * line, 8), TL), :],
            ],
            axis=0,
        )

    get_oct.wait()
    get_par.wait()

    def body(m, carry):
        y = jnp.concatenate([polar(2 * m), polar(2 * m + 1)], axis=1)
        hi, lo = split(y)
        f = jnp.dot(th, jnp.concatenate([hi, lo, hi], axis=0), preferred_element_type=F32)
        for k in range(2):
            n = 2 * m + k
            tab = pl.multiple_of(oct_ref[n] * pitch, 8)
            par = pl.multiple_of(par_ref[0, n] * 8, 8)
            lanes = slice(k * LANES, (k + 1) * LANES)
            values = [
                f[8 * d:8 * d + 8, lanes] * ct_ref[pl.ds(tab + 8 * d, 8), :]
                + f[rows + 8 * d:rows + 8 * d + 8, lanes] * st_ref[pl.ds(tab + 8 * d, 8), :]
                for d in range(rows // 8)
            ]
            values = [value + out_ref[d, pl.ds(par, 8), :] for d, value in enumerate(values)]
            for d, value in enumerate(values):
                out_ref[d, pl.ds(par, 8), :] = value
        return carry

    lax.fori_loop(0, leaves // 2, body, 0, unroll=8)
    for put in puts:
        put.wait()


def aggregate(pattern, octs, parents, theta, phi, angle, dirs):
    leaves = pattern.shape[1]
    edge = jax.ShapeDtypeStruct((2, REACH, pattern.shape[2]), F32)
    return pl.pallas_call(
        aggregate_kernel,
        out_shape=(jax.ShapeDtypeStruct((dirs, PAR_DEV * 8, LANES), F32), edge, edge),
        in_specs=[HBM] * 6,
        out_specs=(VMEM, HBM, HBM),
        scratch_shapes=[
            pltpu.SMEM(octs.shape, I32),
            pltpu.SMEM(parents.shape, I32),
            pltpu.VMEM(pattern.shape, F32),
            pltpu.VMEM(theta.shape, F32),
            pltpu.VMEM(phi.shape, F32),
            pltpu.VMEM(angle.shape, F32),
            pltpu.VMEM(((TL + PAD) * 2 * leaves, LANES), F32),
            pltpu.VMEM((8 * (2 * TT + PAD), LANES), F32),
            pltpu.VMEM((8 * (2 * TT + PAD), LANES), F32),
            pltpu.SemaphoreType.DMA((8,)),
        ],
        compiler_params=pltpu.CompilerParams(vmem_limit_bytes=60 * MIB),
        cost_estimate=estimate(5),
        name="aggregate",
    )(octs, parents, pattern, theta, phi, angle)


def top_kernel(
    src_ref, type_ref, own_hbm, mate_hbm, cross_hbm, table_hbm, out_ref, box_ref, table_ref, tab_ref, one_ref, two_ref, sem
):
    span = own_hbm.shape[0]
    boxes = span // 8
    entries = src_ref.shape[0] // boxes
    gets = [
        pltpu.make_async_copy(source, target, sem.at[i])
        for i, (source, target) in enumerate(
            (
                (table_hbm, table_ref),
                (own_hbm, box_ref.at[0:span, :]),
                (mate_hbm, box_ref.at[span:2 * span, :]),
                (cross_hbm, box_ref.at[2 * span:3 * span, :]),
            )
        )
    ]
    for get in gets:
        get.start()
    gets[0].wait()
    for t in range(table_ref.shape[0] // 8):
        tile = table_ref[8 * t:8 * t + 8, :]
        tab_ref[16 * t:16 * t + 8, :] = tile
        tab_ref[16 * t + 8:16 * t + 16, :] = exchange(tile)
    for get in gets[1:]:
        get.wait()
    together = 8

    def body(m, carry):
        one = [jnp.zeros((8, LANES), F32) for _ in range(together)]
        two = [jnp.zeros((8, LANES), F32) for _ in range(together)]
        for j in range(entries):
            for k in range(together):
                s = pl.multiple_of(src_ref[j * boxes + m * together + k], 8)
                t = pl.multiple_of(type_ref[j * boxes + m * together + k], 16)
                a = box_ref[pl.ds(s, 8), :]
                one[k] = one[k] + a * tab_ref[pl.ds(t, 8), :]
                two[k] = two[k] + a * tab_ref[pl.ds(t + 8, 8), :]
        for k in range(together):
            at = pl.ds(pl.multiple_of(8 * (m * together + k), 8), 8)
            one_ref[at, :] = one[k]
            two_ref[at, :] = two[k]
        return carry

    lax.fori_loop(0, boxes // together, body, 0)
    for r in range(0, boxes, 8):
        for c in range(4):
            lanes = slice(c * LANES, (c + 1) * LANES)
            even = pl.ds(8 * r + 2 * c, 8, stride=8)
            odd = pl.ds(8 * r + 2 * c + 1, 8, stride=8)
            out_ref[0, r:r + 8, lanes] = one_ref[even, :] - one_ref[odd, :]
            out_ref[1, r:r + 8, lanes] = two_ref[even, :] + two_ref[odd, :]


def top_translate(src, kind, own, mate, cross, table):
    rows = own.shape[0]
    return pl.pallas_call(
        top_kernel,
        out_shape=jax.ShapeDtypeStruct((2, rows // 8, 4 * LANES), F32),
        in_specs=[SMEM, SMEM, HBM, HBM, HBM, HBM],
        out_specs=VMEM,
        scratch_shapes=[
            pltpu.VMEM((3 * rows, LANES), F32),
            pltpu.VMEM(table.shape, F32),
            pltpu.VMEM((2 * table.shape[0], LANES), F32),
            pltpu.VMEM((rows, LANES), F32),
            pltpu.VMEM((rows, LANES), F32),
            pltpu.SemaphoreType.DMA((4,)),
        ],
        compiler_params=pltpu.CompilerParams(vmem_limit_bytes=24 * MIB),
        cost_estimate=estimate(9),
        name="top_translate",
    )(src, kind, own, mate, cross, table)


def leaf_kernel(
    src_hbm,
    type_hbm,
    own_hbm,
    pair_a_hbm,
    pair_b_hbm,
    table_hbm,
    after_hbm,
    out_ref,
    src_ref,
    type_ref,
    near_ref,
    tab_ref,
    leaf_ref,
    one_ref,
    two_ref,
    sem,
):
    leaves = own_hbm.shape[1]
    reach = pair_a_hbm.shape[1]
    chunks = own_hbm.shape[2] // LANES
    size = 2 * chunks
    pitch = 2 * size + PAD
    odd = lax.axis_index("dir") % 2
    after = reach + leaves
    place_a = pl.multiple_of((1 - odd) * after, 8)
    place_b = pl.multiple_of(odd * after, 8)
    gets = [
        pltpu.make_async_copy(source, target, sem.at[i])
        for i, (source, target) in enumerate(
            (
                (table_hbm, tab_ref),
                (own_hbm, near_ref.at[:, reach:after, :]),
                (pair_a_hbm, near_ref.at[:, pl.ds(place_a, reach), :]),
                (pair_b_hbm, near_ref.at[:, pl.ds(place_b, reach), :]),
                (src_hbm, src_ref),
                (type_hbm, type_ref),
            )
        )
    ]
    for get in gets:
        get.start()
    for get in gets[1:4]:
        get.wait()
    for first in range(0, near_ref.shape[1], 8):
        for c in range(chunks):
            lanes = slice(c * LANES, (c + 1) * LANES)
            real = near_ref[0, first:first + 8, lanes]
            imag = near_ref[1, first:first + 8, lanes]
            at = first * pitch + 2 * c
            leaf_ref[pl.ds(at, 8, stride=pitch), :] = real
            leaf_ref[pl.ds(at + 1, 8, stride=pitch), :] = imag
            leaf_ref[pl.ds(at + size, 8, stride=pitch), :] = imag
            leaf_ref[pl.ds(at + size + 1, 8, stride=pitch), :] = real
    for get in gets[:1] + gets[4:]:
        get.wait()
    line = size + PAD

    def body(i, carry):
        one = jnp.zeros((size, LANES), F32)
        two = jnp.zeros((size, LANES), F32)
        for j in range(src_ref.shape[0]):
            s = pl.multiple_of(src_ref[j, i], 8)
            t = pl.multiple_of(type_ref[j, i], size)
            tab = tab_ref[pl.ds(t, size), :]
            one = one + tab * leaf_ref[pl.ds(s, size), :]
            two = two + tab * leaf_ref[pl.ds(s + size, size), :]
        at = pl.ds(pl.multiple_of(i * line, 8), size)
        one_ref[at, :] = one
        two_ref[at, :] = two
        return carry

    lax.fori_loop(0, leaves, body, 0)
    for first in range(0, leaves, 8):
        for c in range(chunks):
            lanes = slice(c * LANES, (c + 1) * LANES)
            even = pl.ds(first * line + 2 * c, 8, stride=line)
            odd = pl.ds(first * line + 2 * c + 1, 8, stride=line)
            out_ref[0, first:first + 8, lanes] = one_ref[even, :] - one_ref[odd, :]
            out_ref[1, first:first + 8, lanes] = two_ref[even, :] + two_ref[odd, :]


def leaf_translate(src, kind, own, pair_a, pair_b, table, after):
    leaves = own.shape[1]
    reach = pair_a.shape[1]
    size = 2 * own.shape[2] // LANES
    line = size + PAD
    near = leaves + 2 * reach
    return pl.pallas_call(
        leaf_kernel,
        out_shape=jax.ShapeDtypeStruct(own.shape, F32),
        in_specs=[HBM] * 7,
        out_specs=VMEM,
        scratch_shapes=[
            pltpu.SMEM(src.shape, I32),
            pltpu.SMEM(kind.shape, I32),
            pltpu.VMEM((2, near, own.shape[2]), F32),
            pltpu.VMEM(table.shape, F32),
            pltpu.VMEM((near * (2 * size + PAD), LANES), F32),
            pltpu.VMEM((leaves * line, LANES), F32),
            pltpu.VMEM((leaves * line, LANES), F32),
            pltpu.SemaphoreType.DMA((6,)),
        ],
        compiler_params=pltpu.CompilerParams(vmem_limit_bytes=60 * MIB),
        cost_estimate=estimate(5),
        name="leaf_translate",
    )(src, kind, own, pair_a, pair_b, table, after)


def interleaved(table):
    types = table.shape[1]
    view = table.reshape(2, types, -1, LANES)
    return view.transpose(1, 2, 0, 3).reshape(-1, LANES)


def per_device(
    leaf_pattern,
    leaf_parent,
    octant,
    interp_theta,
    interp_phi,
    shift_angle,
    near_src,
    near_type,
    leaf_transfer,
    inter_src,
    inter_type,
    top_transfer,
):
    leaves = leaf_pattern.shape[1]
    dirs = lax.axis_size("dir")
    groups = lax.axis_size("box")
    box = lax.axis_index("box")
    parents, edge_b, edge_a = aggregate(
        leaf_pattern, octant, leaf_parent, interp_theta.T, interp_phi.T, shift_angle, dirs
    )
    directed = lax.all_to_all(parents, "dir", split_axis=0, concat_axis=0)
    count = dirs * groups
    pair_a = lax.ppermute(edge_a, ("box", "dir"), [(i, i ^ 1) for i in range(count)])
    pair_b = lax.ppermute(edge_b, ("box", "dir"), [(i, ((i + 1) ^ 1) - 1) for i in range(1, count - 1)])

    own = directed.reshape(-1, LANES)
    boxes = inter_src.shape[0]
    mate = lax.ppermute(own, "box", [(i, i ^ 1) for i in range(groups)])
    cross = lax.ppermute(own, "box", [(i, ((i + 1) ^ 1) - 1) for i in range(1, groups - 1)])
    src = inter_src.T
    group = src // boxes
    place = jnp.where(group == box, 0, jnp.where(group == (box ^ 1), boxes, 2 * boxes)) + src % boxes
    top_src = (place * 8).reshape(-1)
    top_type = (inter_type.T * 16).reshape(-1)
    incoming = top_translate(top_src, top_type, own, mate, cross, interleaved(top_transfer))

    size = 2 * leaf_pattern.shape[2] // LANES
    first_leaf = lax.axis_index(("box", "dir")) * leaves
    leaf_src = (near_src.T - (first_leaf - REACH)) * (2 * size + PAD)
    leaf_incoming = leaf_translate(
        leaf_src, near_type.T * size, leaf_pattern, pair_a, pair_b, interleaved(leaf_transfer), directed
    )
    return (incoming, leaf_incoming)


def solution(mesh):
    return jax.shard_map(
        per_device,
        mesh=mesh,
        in_specs=(
            P(None, ("box", "dir"), None),
            P(("box", "dir"), None),
            P(("box", "dir")),
            P(),
            P(),
            P(),
            P(("box", "dir"), None),
            P(("box", "dir"), None),
            P(),
            P("box", None),
            P("box", None),
            P(None, None, "dir"),
        ),
        out_specs=(P(None, "box", "dir"), P(None, ("box", "dir"), None)),
        check_vma=False,
    )
```

```python
import jax
import jax.numpy as jnp
from jax import lax
from jax.experimental import pallas as pl
from jax.experimental.pallas import tpu as pltpu
from jax.sharding import PartitionSpec as P

TL = 32
PL = 64
TT = 64
PT = 128
PAR_DEV = 8
REACH = 16
LANES = 128
PAD = 8
F32 = jnp.float32
BF16 = jnp.bfloat16
I32 = jnp.int32
MIB = 1024 * 1024
VMEM = pl.BlockSpec(memory_space=pltpu.VMEM)
SMEM = pl.BlockSpec(memory_space=pltpu.SMEM)
HBM = pl.BlockSpec(memory_space=pltpu.HBM)
ANY = pl.BlockSpec(memory_space=pl.ANY)


def split(x):
    hi = x.astype(BF16)
    lo = (x - hi.astype(F32)).astype(BF16)
    return hi, lo


def cos_sin(x):
    turns = jnp.round(x * 0.63661977236758134)
    r = (x - turns * 1.5703125) - turns * 4.83826794896619e-4
    z = r * r
    s = r + r * z * (-1.6666654611e-1 + z * (8.3321608736e-3 + z * -1.9515295891e-4))
    c = 1.0 - 0.5 * z + z * z * (4.166664568298827e-2 + z * (-1.388731625493765e-3 + z * 2.443315711809948e-5))
    size = jnp.abs(turns)
    odd = size == 1.0
    half = size == 2.0
    big_c = jnp.where(odd, s, c)
    big_s = jnp.where(odd, c, s)
    cosine = jnp.where(half | (turns == 1.0), -big_c, big_c)
    sine = jnp.where(half | (turns == -1.0), -big_s, big_s)
    return cosine, sine


def exchange(x):
    even = lax.broadcasted_iota(I32, x.shape, 0) % 2 == 0
    return jnp.where(even, pltpu.roll(x, x.shape[0] - 1, 0), pltpu.roll(x, 1, 0))


def estimate(microseconds):
    return pl.CostEstimate(flops=1000, bytes_accessed=int(microseconds * 3_000_000), transcendentals=0)


def aggregate_kernel(
    oct_hbm,
    par_hbm,
    x_hbm,
    theta_hbm,
    phi_hbm,
    angle_hbm,
    out_ref,
    edge_b_hbm,
    edge_a_hbm,
    oct_ref,
    par_ref,
    x_ref,
    theta_ref,
    phi_ref,
    angle_ref,
    y_ref,
    ct_ref,
    st_ref,
    sem,
):
    leaves = x_ref.shape[1]
    rows = 2 * TT
    pitch = rows + PAD
    line = TL + PAD
    reach = edge_b_hbm.shape[1]
    gets = [
        pltpu.make_async_copy(source, target, sem.at[i])
        for i, (source, target) in enumerate(
            (
                (angle_hbm, angle_ref),
                (theta_hbm, theta_ref),
                (phi_hbm, phi_ref),
                (x_hbm, x_ref),
                (oct_hbm, oct_ref),
                (par_hbm, par_ref),
            )
        )
    ]
    last = leaves - reach
    start_a = pl.multiple_of(jnp.where(lax.axis_index("dir") % 2 == 0, last, 0), 8)
    start_b = pl.multiple_of(last - start_a, 8)
    puts = [
        pltpu.make_async_copy(x_ref.at[:, pl.ds(start_b, reach), :], edge_b_hbm, sem.at[6]),
        pltpu.make_async_copy(x_ref.at[:, pl.ds(start_a, reach), :], edge_a_hbm, sem.at[7]),
    ]
    for get in gets:
        get.start()
    get_angle, get_theta, get_phi, get_x, get_oct, get_par = gets
    out_ref[...] = jnp.zeros_like(out_ref)
    get_angle.wait()
    for s in range(TT):
        cosine, sine = cos_sin(angle_ref[:, s * LANES:(s + 1) * LANES])
        ct_ref[pl.ds(2 * s, 8, stride=pitch), :] = cosine
        ct_ref[pl.ds(2 * s + 1, 8, stride=pitch), :] = cosine
        st_ref[pl.ds(2 * s, 8, stride=pitch), :] = -sine
        st_ref[pl.ds(2 * s + 1, 8, stride=pitch), :] = sine
    get_theta.wait()
    hi, lo = split(theta_ref[...])
    stack = jnp.concatenate([hi, hi, hi, hi, lo, lo], axis=0)
    row = lax.broadcasted_iota(jnp.int32, (rows, TT), 0)
    col = lax.broadcasted_iota(jnp.int32, (rows, TT), 1)
    pick = jnp.where(row // 2 == col, 1.0, 0.0).astype(BF16)
    dims = (((1,), (1,)), ((), ()))
    wide = lax.dot_general(pick, stack, dims, preferred_element_type=F32)
    row = lax.broadcasted_iota(jnp.int32, wide.shape, 0)
    col = lax.broadcasted_iota(jnp.int32, wide.shape, 1)
    same = row % 2 == (col // TL) % 2
    th = jnp.concatenate([jnp.where(same, wide, 0.0), jnp.where(same, 0.0, wide)], axis=0).astype(BF16)
    get_phi.wait()
    phi = phi_ref[...]
    zero = jnp.zeros_like(phi)
    pair = jnp.concatenate([jnp.concatenate([phi, zero], axis=1), jnp.concatenate([zero, phi], axis=1)], axis=0)
    ph_hi, ph_lo = split(pair)
    ph_two = jnp.concatenate([ph_hi, ph_hi], axis=0)
    get_x.wait()
    for put in puts:
        put.start()
    for u in range(TL // 2):
        lanes = slice(u * LANES, (u + 1) * LANES)
        block = jnp.concatenate([x_ref[0, :, lanes], x_ref[1, :, lanes]], axis=0)
        hi, lo = split(block)
        y = jnp.dot(jnp.concatenate([hi, lo], axis=1), ph_two, preferred_element_type=F32) + jnp.dot(
            hi, ph_lo, preferred_element_type=F32
        )
        for g in range(0, 2 * leaves, 8):
            y_ref[pl.ds(g * line + 2 * u, 8, stride=line), :] = y[g:g + 8, :LANES]
            y_ref[pl.ds(g * line + 2 * u + 1, 8, stride=line), :] = y[g:g + 8, LANES:]

    def polar(n):
        return jnp.concatenate(
            [
                y_ref[pl.ds(pl.multiple_of(n * line, 8), TL), :],
                y_ref[pl.ds(pl.multiple_of((leaves + n) * line, 8), TL), :],
            ],
            axis=0,
        )

    get_oct.wait()
    get_par.wait()

    def body(m, carry):
        y = jnp.concatenate([polar(2 * m), polar(2 * m + 1)], axis=1)
        hi, lo = split(y)
        f = jnp.dot(th, jnp.concatenate([hi, lo, hi], axis=0), preferred_element_type=F32)
        for k in range(2):
            n = 2 * m + k
            tab = pl.multiple_of(oct_ref[n] * pitch, 8)
            par = pl.multiple_of(par_ref[0, n] * 8, 8)
            lanes = slice(k * LANES, (k + 1) * LANES)
            values = [
                f[8 * d:8 * d + 8, lanes] * ct_ref[pl.ds(tab + 8 * d, 8), :]
                + f[rows + 8 * d:rows + 8 * d + 8, lanes] * st_ref[pl.ds(tab + 8 * d, 8), :]
                for d in range(rows // 8)
            ]
            values = [value + out_ref[d, pl.ds(par, 8), :] for d, value in enumerate(values)]
            for d, value in enumerate(values):
                out_ref[d, pl.ds(par, 8), :] = value
        return carry

    lax.fori_loop(0, leaves // 2, body, 0, unroll=8)
    for put in puts:
        put.wait()


def aggregate(pattern, octs, parents, theta, phi, angle, dirs):
    leaves = pattern.shape[1]
    edge = jax.ShapeDtypeStruct((2, REACH, pattern.shape[2]), F32)
    return pl.pallas_call(
        aggregate_kernel,
        out_shape=(jax.ShapeDtypeStruct((dirs, PAR_DEV * 8, LANES), F32), edge, edge),
        in_specs=[HBM] * 6,
        out_specs=(VMEM, HBM, HBM),
        scratch_shapes=[
            pltpu.SMEM(octs.shape, I32),
            pltpu.SMEM(parents.shape, I32),
            pltpu.VMEM(pattern.shape, F32),
            pltpu.VMEM(theta.shape, F32),
            pltpu.VMEM(phi.shape, F32),
            pltpu.VMEM(angle.shape, F32),
            pltpu.VMEM(((TL + PAD) * 2 * leaves, LANES), F32),
            pltpu.VMEM((8 * (2 * TT + PAD), LANES), F32),
            pltpu.VMEM((8 * (2 * TT + PAD), LANES), F32),
            pltpu.SemaphoreType.DMA((8,)),
        ],
        compiler_params=pltpu.CompilerParams(vmem_limit_bytes=60 * MIB),
        cost_estimate=estimate(5),
        name="aggregate",
    )(octs, parents, pattern, theta, phi, angle)


def top_kernel(
    src_ref, type_ref, own_hbm, mate_hbm, cross_hbm, table_hbm, out_hbm, out_ref, box_ref, table_ref, tab_ref, one_ref, two_ref, sem
):
    span = own_hbm.shape[0]
    boxes = span // 8
    entries = src_ref.shape[0] // boxes
    gets = [
        pltpu.make_async_copy(source, target, sem.at[i])
        for i, (source, target) in enumerate(
            (
                (table_hbm, table_ref),
                (own_hbm, box_ref.at[0:span, :]),
                (mate_hbm, box_ref.at[span:2 * span, :]),
                (cross_hbm, box_ref.at[2 * span:3 * span, :]),
            )
        )
    ]
    for get in gets:
        get.start()
    gets[0].wait()
    for t in range(table_ref.shape[0] // 8):
        tile = table_ref[8 * t:8 * t + 8, :]
        tab_ref[16 * t:16 * t + 8, :] = tile
        tab_ref[16 * t + 8:16 * t + 16, :] = exchange(tile)
    for get in gets[1:]:
        get.wait()
    together = 8

    def body(m, carry):
        one = [jnp.zeros((8, LANES), F32) for _ in range(together)]
        two = [jnp.zeros((8, LANES), F32) for _ in range(together)]
        for j in range(entries):
            for k in range(together):
                s = pl.multiple_of(src_ref[j * boxes + m * together + k], 8)
                t = pl.multiple_of(type_ref[j * boxes + m * together + k], 16)
                a = box_ref[pl.ds(s, 8), :]
                one[k] = one[k] + a * tab_ref[pl.ds(t, 8), :]
                two[k] = two[k] + a * tab_ref[pl.ds(t + 8, 8), :]
        for k in range(together):
            at = pl.ds(pl.multiple_of(8 * (m * together + k), 8), 8)
            one_ref[at, :] = one[k]
            two_ref[at, :] = two[k]
        return carry

    steps = boxes // together
    parts = 4
    puts = []
    for q in range(parts):
        lax.fori_loop(q * steps // parts, (q + 1) * steps // parts, body, 0)
        start = q * boxes // parts
        for r in range(start, start + boxes // parts, 8):
            for c in range(4):
                lanes = slice(c * LANES, (c + 1) * LANES)
                even = pl.ds(8 * r + 2 * c, 8, stride=8)
                odd = pl.ds(8 * r + 2 * c + 1, 8, stride=8)
                out_ref[0, r:r + 8, lanes] = one_ref[even, :] - one_ref[odd, :]
                out_ref[1, r:r + 8, lanes] = two_ref[even, :] + two_ref[odd, :]
        rows = slice(start, start + boxes // parts)
        puts.append(pltpu.make_async_copy(out_ref.at[:, rows, :], out_hbm.at[:, rows, :], sem.at[4 + q]))
        puts[q].start()
    for put in puts:
        put.wait()


def top_translate(src, kind, own, mate, cross, table):
    rows = own.shape[0]
    return pl.pallas_call(
        top_kernel,
        out_shape=jax.ShapeDtypeStruct((2, rows // 8, 4 * LANES), F32),
        in_specs=[SMEM, SMEM, HBM, HBM, HBM, HBM],
        out_specs=HBM,
        scratch_shapes=[
            pltpu.VMEM((2, rows // 8, 4 * LANES), F32),
            pltpu.VMEM((3 * rows, LANES), F32),
            pltpu.VMEM(table.shape, F32),
            pltpu.VMEM((2 * table.shape[0], LANES), F32),
            pltpu.VMEM((rows, LANES), F32),
            pltpu.VMEM((rows, LANES), F32),
            pltpu.SemaphoreType.DMA((8,)),
        ],
        compiler_params=pltpu.CompilerParams(vmem_limit_bytes=24 * MIB),
        cost_estimate=estimate(9),
        name="top_translate",
    )(src, kind, own, mate, cross, table)


def leaf_kernel(
    src_hbm,
    type_hbm,
    own_hbm,
    pair_a_hbm,
    pair_b_hbm,
    table_hbm,
    out_hbm,
    out_ref,
    src_ref,
    type_ref,
    near_ref,
    tab_ref,
    leaf_ref,
    one_ref,
    two_ref,
    sem,
):
    leaves = own_hbm.shape[1]
    reach = pair_a_hbm.shape[1]
    chunks = own_hbm.shape[2] // LANES
    size = 2 * chunks
    pitch = 2 * size + PAD
    side = lax.axis_index("dir") % 2
    after = reach + leaves
    place_a = pl.multiple_of((1 - side) * after, 8)
    place_b = pl.multiple_of(side * after, 8)
    gets = [
        pltpu.make_async_copy(source, target, sem.at[i])
        for i, (source, target) in enumerate(
            (
                (table_hbm, tab_ref),
                (own_hbm, near_ref.at[:, reach:after, :]),
                (pair_a_hbm, near_ref.at[:, pl.ds(place_a, reach), :]),
                (pair_b_hbm, near_ref.at[:, pl.ds(place_b, reach), :]),
                (src_hbm, src_ref),
                (type_hbm, type_ref),
            )
        )
    ]
    for get in gets:
        get.start()
    for get in gets[1:4]:
        get.wait()
    for first in range(0, near_ref.shape[1], 8):
        for c in range(chunks):
            lanes = slice(c * LANES, (c + 1) * LANES)
            real = near_ref[0, first:first + 8, lanes]
            imag = near_ref[1, first:first + 8, lanes]
            at = first * pitch + 2 * c
            leaf_ref[pl.ds(at, 8, stride=pitch), :] = real
            leaf_ref[pl.ds(at + 1, 8, stride=pitch), :] = imag
            leaf_ref[pl.ds(at + size, 8, stride=pitch), :] = imag
            leaf_ref[pl.ds(at + size + 1, 8, stride=pitch), :] = real
    for get in gets[:1] + gets[4:]:
        get.wait()
    line = size + PAD

    def body(i, carry):
        one = jnp.zeros((size, LANES), F32)
        two = jnp.zeros((size, LANES), F32)
        for j in range(src_ref.shape[0]):
            s = pl.multiple_of(src_ref[j, i], 8)
            t = pl.multiple_of(type_ref[j, i], size)
            tab = tab_ref[pl.ds(t, size), :]
            one = one + tab * leaf_ref[pl.ds(s, size), :]
            two = two + tab * leaf_ref[pl.ds(s + size, size), :]
        at = pl.ds(pl.multiple_of(i * line, 8), size)
        one_ref[at, :] = one
        two_ref[at, :] = two
        return carry

    parts = 3
    puts = []
    for q in range(parts):
        start = q * leaves // parts
        rows = slice(start, start + leaves // parts)
        lax.fori_loop(rows.start, rows.stop, body, 0)
        for first in range(rows.start, rows.stop, 8):
            for c in range(chunks):
                lanes = slice(c * LANES, (c + 1) * LANES)
                even = pl.ds(first * line + 2 * c, 8, stride=line)
                odd = pl.ds(first * line + 2 * c + 1, 8, stride=line)
                out_ref[0, first:first + 8, lanes] = one_ref[even, :] - one_ref[odd, :]
                out_ref[1, first:first + 8, lanes] = two_ref[even, :] + two_ref[odd, :]
        puts.append(pltpu.make_async_copy(out_ref.at[:, rows, :], out_hbm.at[:, rows, :], sem.at[6 + q]))
        puts[q].start()
    for put in puts:
        put.wait()


def leaf_translate(src, kind, own, pair_a, pair_b, table):
    leaves = own.shape[1]
    reach = pair_a.shape[1]
    size = 2 * own.shape[2] // LANES
    line = size + PAD
    near = leaves + 2 * reach
    return pl.pallas_call(
        leaf_kernel,
        out_shape=jax.ShapeDtypeStruct(own.shape, F32),
        in_specs=[ANY, ANY, HBM, ANY, ANY, HBM],
        out_specs=HBM,
        scratch_shapes=[
            pltpu.VMEM(own.shape, F32),
            pltpu.SMEM(src.shape, I32),
            pltpu.SMEM(kind.shape, I32),
            pltpu.VMEM((2, near, own.shape[2]), F32),
            pltpu.VMEM(table.shape, F32),
            pltpu.VMEM((near * (2 * size + PAD), LANES), F32),
            pltpu.VMEM((leaves * line, LANES), F32),
            pltpu.VMEM((leaves * line, LANES), F32),
            pltpu.SemaphoreType.DMA((9,)),
        ],
        compiler_params=pltpu.CompilerParams(vmem_limit_bytes=53 * MIB),
        cost_estimate=estimate(5),
        name="leaf_translate",
    )(src, kind, own, pair_a, pair_b, table)


def interleaved(table):
    types = table.shape[1]
    view = table.reshape(2, types, -1, LANES)
    return view.transpose(1, 2, 0, 3).reshape(-1, LANES)


def per_device(
    leaf_pattern,
    leaf_parent,
    octant,
    interp_theta,
    interp_phi,
    shift_angle,
    near_src,
    near_type,
    leaf_transfer,
    inter_src,
    inter_type,
    top_transfer,
):
    leaves = leaf_pattern.shape[1]
    dirs = lax.axis_size("dir")
    groups = lax.axis_size("box")
    box = lax.axis_index("box")
    parents, edge_b, edge_a = aggregate(
        leaf_pattern, octant, leaf_parent, interp_theta.T, interp_phi.T, shift_angle, dirs
    )
    directed = lax.all_to_all(parents, "dir", split_axis=0, concat_axis=0)
    count = dirs * groups
    pair_a = lax.ppermute(edge_a, ("box", "dir"), [(i, i ^ 1) for i in range(count)])
    pair_b = lax.ppermute(edge_b, ("box", "dir"), [(i, ((i + 1) ^ 1) - 1) for i in range(1, count - 1)])

    own = directed.reshape(-1, LANES)
    boxes = inter_src.shape[0]
    mate = lax.ppermute(own, "box", [(i, i ^ 1) for i in range(groups)])
    cross = lax.ppermute(own, "box", [(i, ((i + 1) ^ 1) - 1) for i in range(1, groups - 1)])
    src = inter_src.T
    group = src // boxes
    place = jnp.where(group == box, 0, jnp.where(group == (box ^ 1), boxes, 2 * boxes)) + src % boxes
    top_src = (place * 8).reshape(-1)
    top_type = (inter_type.T * 16).reshape(-1)
    incoming = top_translate(top_src, top_type, own, mate, cross, interleaved(top_transfer))

    size = 2 * leaf_pattern.shape[2] // LANES
    first_leaf = lax.axis_index(("box", "dir")) * leaves
    leaf_src = (near_src.T - (first_leaf - REACH)) * (2 * size + PAD)
    leaf_incoming = leaf_translate(
        leaf_src, near_type.T * size, leaf_pattern, pair_a, pair_b, interleaved(leaf_transfer)
    )
    return (incoming, leaf_incoming)


def solution(mesh):
    return jax.shard_map(
        per_device,
        mesh=mesh,
        in_specs=(
            P(None, ("box", "dir"), None),
            P(("box", "dir"), None),
            P(("box", "dir")),
            P(),
            P(),
            P(),
            P(("box", "dir"), None),
            P(("box", "dir"), None),
            P(),
            P("box", None),
            P("box", None),
            P(None, None, "dir"),
        ),
        out_specs=(P(None, "box", "dir"), P(None, ("box", "dir"), None)),
        check_vma=False,
    )
```

```python
import jax
import jax.numpy as jnp
from jax import lax
from jax.experimental import pallas as pl
from jax.experimental.pallas import tpu as pltpu
from jax.sharding import PartitionSpec as P

TL = 32
PL = 64
TT = 64
PT = 128
PAR_DEV = 8
REACH = 16
LANES = 128
PAD = 8
F32 = jnp.float32
BF16 = jnp.bfloat16
I32 = jnp.int32
MIB = 1024 * 1024
VMEM = pl.BlockSpec(memory_space=pltpu.VMEM)
SMEM = pl.BlockSpec(memory_space=pltpu.SMEM)
HBM = pl.BlockSpec(memory_space=pltpu.HBM)
ANY = pl.BlockSpec(memory_space=pl.ANY)


def split(x):
    hi = x.astype(BF16)
    lo = (x - hi.astype(F32)).astype(BF16)
    return hi, lo


def cos_sin(x):
    turns = jnp.round(x * 0.63661977236758134)
    r = (x - turns * 1.5703125) - turns * 4.83826794896619e-4
    z = r * r
    s = r + r * z * (-1.6666654611e-1 + z * (8.3321608736e-3 + z * -1.9515295891e-4))
    c = 1.0 - 0.5 * z + z * z * (4.166664568298827e-2 + z * (-1.388731625493765e-3 + z * 2.443315711809948e-5))
    size = jnp.abs(turns)
    odd = size == 1.0
    half = size == 2.0
    big_c = jnp.where(odd, s, c)
    big_s = jnp.where(odd, c, s)
    cosine = jnp.where(half | (turns == 1.0), -big_c, big_c)
    sine = jnp.where(half | (turns == -1.0), -big_s, big_s)
    return cosine, sine


def exchange(x):
    even = lax.broadcasted_iota(I32, x.shape, 0) % 2 == 0
    return jnp.where(even, pltpu.roll(x, x.shape[0] - 1, 0), pltpu.roll(x, 1, 0))


def estimate(microseconds):
    return pl.CostEstimate(flops=1000, bytes_accessed=int(microseconds * 3_000_000), transcendentals=0)


def aggregate_kernel(
    oct_hbm,
    par_hbm,
    x_hbm,
    theta_hbm,
    phi_hbm,
    angle_hbm,
    out_ref,
    edge_b_hbm,
    edge_a_hbm,
    oct_ref,
    par_ref,
    x_ref,
    theta_ref,
    phi_ref,
    angle_ref,
    y_ref,
    ct_ref,
    st_ref,
    sem,
):
    leaves = x_ref.shape[1]
    rows = 2 * TT
    pitch = rows + PAD
    line = TL + PAD
    reach = edge_b_hbm.shape[1]
    gets = [
        pltpu.make_async_copy(source, target, sem.at[i])
        for i, (source, target) in enumerate(
            (
                (angle_hbm, angle_ref),
                (theta_hbm, theta_ref),
                (phi_hbm, phi_ref),
                (x_hbm, x_ref),
                (oct_hbm, oct_ref),
                (par_hbm, par_ref),
            )
        )
    ]
    last = leaves - reach
    start_a = pl.multiple_of(jnp.where(lax.axis_index("dir") % 2 == 0, last, 0), 8)
    start_b = pl.multiple_of(last - start_a, 8)
    puts = [
        pltpu.make_async_copy(x_ref.at[:, pl.ds(start_b, reach), :], edge_b_hbm, sem.at[6]),
        pltpu.make_async_copy(x_ref.at[:, pl.ds(start_a, reach), :], edge_a_hbm, sem.at[7]),
    ]
    for get in gets:
        get.start()
    get_angle, get_theta, get_phi, get_x, get_oct, get_par = gets
    out_ref[...] = jnp.zeros_like(out_ref)
    get_angle.wait()
    for s in range(TT):
        cosine, sine = cos_sin(angle_ref[:, s * LANES:(s + 1) * LANES])
        ct_ref[pl.ds(2 * s, 8, stride=pitch), :] = cosine
        ct_ref[pl.ds(2 * s + 1, 8, stride=pitch), :] = cosine
        st_ref[pl.ds(2 * s, 8, stride=pitch), :] = -sine
        st_ref[pl.ds(2 * s + 1, 8, stride=pitch), :] = sine
    get_theta.wait()
    hi, lo = split(theta_ref[...])
    stack = jnp.concatenate([hi, hi, hi, hi, lo, lo], axis=0)
    row = lax.broadcasted_iota(jnp.int32, (rows, TT), 0)
    col = lax.broadcasted_iota(jnp.int32, (rows, TT), 1)
    pick = jnp.where(row // 2 == col, 1.0, 0.0).astype(BF16)
    dims = (((1,), (1,)), ((), ()))
    wide = lax.dot_general(pick, stack, dims, preferred_element_type=F32)
    row = lax.broadcasted_iota(jnp.int32, wide.shape, 0)
    col = lax.broadcasted_iota(jnp.int32, wide.shape, 1)
    same = row % 2 == (col // TL) % 2
    th = jnp.concatenate([jnp.where(same, wide, 0.0), jnp.where(same, 0.0, wide)], axis=0).astype(BF16)
    get_phi.wait()
    phi = phi_ref[...]
    zero = jnp.zeros_like(phi)
    pair = jnp.concatenate([jnp.concatenate([phi, zero], axis=1), jnp.concatenate([zero, phi], axis=1)], axis=0)
    ph_hi, ph_lo = split(pair)
    ph_two = jnp.concatenate([ph_hi, ph_hi], axis=0)
    get_x.wait()
    for put in puts:
        put.start()
    for u in range(TL // 2):
        lanes = slice(u * LANES, (u + 1) * LANES)
        block = jnp.concatenate([x_ref[0, :, lanes], x_ref[1, :, lanes]], axis=0)
        hi, lo = split(block)
        y = jnp.dot(jnp.concatenate([hi, lo], axis=1), ph_two, preferred_element_type=F32) + jnp.dot(
            hi, ph_lo, preferred_element_type=F32
        )
        for g in range(0, 2 * leaves, 8):
            y_ref[pl.ds(g * line + 2 * u, 8, stride=line), :] = y[g:g + 8, :LANES]
            y_ref[pl.ds(g * line + 2 * u + 1, 8, stride=line), :] = y[g:g + 8, LANES:]

    def polar(n):
        return jnp.concatenate(
            [
                y_ref[pl.ds(pl.multiple_of(n * line, 8), TL), :],
                y_ref[pl.ds(pl.multiple_of((leaves + n) * line, 8), TL), :],
            ],
            axis=0,
        )

    get_oct.wait()
    get_par.wait()

    def body(m, carry):
        y = jnp.concatenate([polar(2 * m), polar(2 * m + 1)], axis=1)
        hi, lo = split(y)
        f = jnp.dot(th, jnp.concatenate([hi, lo, hi], axis=0), preferred_element_type=F32)
        for k in range(2):
            n = 2 * m + k
            tab = pl.multiple_of(oct_ref[n] * pitch, 8)
            par = pl.multiple_of(par_ref[0, n] * 8, 8)
            lanes = slice(k * LANES, (k + 1) * LANES)
            values = [
                f[8 * d:8 * d + 8, lanes] * ct_ref[pl.ds(tab + 8 * d, 8), :]
                + f[rows + 8 * d:rows + 8 * d + 8, lanes] * st_ref[pl.ds(tab + 8 * d, 8), :]
                for d in range(rows // 8)
            ]
            values = [value + out_ref[d, pl.ds(par, 8), :] for d, value in enumerate(values)]
            for d, value in enumerate(values):
                out_ref[d, pl.ds(par, 8), :] = value
        return carry

    lax.fori_loop(0, leaves // 2, body, 0, unroll=8)
    for put in puts:
        put.wait()


def aggregate(pattern, octs, parents, theta, phi, angle, dirs):
    leaves = pattern.shape[1]
    edge = jax.ShapeDtypeStruct((2, REACH, pattern.shape[2]), F32)
    return pl.pallas_call(
        aggregate_kernel,
        out_shape=(jax.ShapeDtypeStruct((dirs, PAR_DEV * 8, LANES), F32), edge, edge),
        in_specs=[HBM] * 6,
        out_specs=(VMEM, HBM, HBM),
        scratch_shapes=[
            pltpu.SMEM(octs.shape, I32),
            pltpu.SMEM(parents.shape, I32),
            pltpu.VMEM(pattern.shape, F32),
            pltpu.VMEM(theta.shape, F32),
            pltpu.VMEM(phi.shape, F32),
            pltpu.VMEM(angle.shape, F32),
            pltpu.VMEM(((TL + PAD) * 2 * leaves, LANES), F32),
            pltpu.VMEM((8 * (2 * TT + PAD), LANES), F32),
            pltpu.VMEM((8 * (2 * TT + PAD), LANES), F32),
            pltpu.SemaphoreType.DMA((8,)),
        ],
        compiler_params=pltpu.CompilerParams(vmem_limit_bytes=60 * MIB),
        cost_estimate=estimate(5),
        name="aggregate",
    )(octs, parents, pattern, theta, phi, angle)


def top_kernel(
    src_ref, type_ref, own_hbm, mate_hbm, cross_hbm, table_hbm, out_hbm, out_ref, box_ref, table_ref, tab_ref, one_ref, two_ref, sem
):
    span = own_hbm.shape[0]
    boxes = span // 8
    entries = src_ref.shape[0] // boxes
    gets = [
        pltpu.make_async_copy(source, target, sem.at[i])
        for i, (source, target) in enumerate(
            (
                (table_hbm, table_ref),
                (own_hbm, box_ref.at[0:span, :]),
                (mate_hbm, box_ref.at[span:2 * span, :]),
                (cross_hbm, box_ref.at[2 * span:3 * span, :]),
            )
        )
    ]
    for get in gets:
        get.start()
    gets[0].wait()
    for t in range(table_ref.shape[0] // 8):
        tile = table_ref[8 * t:8 * t + 8, :]
        tab_ref[16 * t:16 * t + 8, :] = tile
        tab_ref[16 * t + 8:16 * t + 16, :] = exchange(tile)
    for get in gets[1:]:
        get.wait()
    together = 8

    def body(m, carry):
        one = [jnp.zeros((8, LANES), F32) for _ in range(together)]
        two = [jnp.zeros((8, LANES), F32) for _ in range(together)]
        for j in range(entries):
            for k in range(together):
                s = pl.multiple_of(src_ref[j * boxes + m * together + k], 8)
                t = pl.multiple_of(type_ref[j * boxes + m * together + k], 16)
                a = box_ref[pl.ds(s, 8), :]
                one[k] = one[k] + a * tab_ref[pl.ds(t, 8), :]
                two[k] = two[k] + a * tab_ref[pl.ds(t + 8, 8), :]
        for k in range(together):
            at = pl.ds(pl.multiple_of(8 * (m * together + k), 8), 8)
            one_ref[at, :] = one[k]
            two_ref[at, :] = two[k]
        return carry

    steps = boxes // together
    parts = 4
    puts = []
    for q in range(parts):
        lax.fori_loop(q * steps // parts, (q + 1) * steps // parts, body, 0)
        start = q * boxes // parts
        for r in range(start, start + boxes // parts, 8):
            for c in range(4):
                lanes = slice(c * LANES, (c + 1) * LANES)
                even = pl.ds(8 * r + 2 * c, 8, stride=8)
                odd = pl.ds(8 * r + 2 * c + 1, 8, stride=8)
                out_ref[0, r:r + 8, lanes] = one_ref[even, :] - one_ref[odd, :]
                out_ref[1, r:r + 8, lanes] = two_ref[even, :] + two_ref[odd, :]
        rows = slice(start, start + boxes // parts)
        puts.append(pltpu.make_async_copy(out_ref.at[:, rows, :], out_hbm.at[:, rows, :], sem.at[4 + q]))
        puts[q].start()
    for put in puts:
        put.wait()


def top_translate(src, kind, own, mate, cross, table):
    rows = own.shape[0]
    return pl.pallas_call(
        top_kernel,
        out_shape=jax.ShapeDtypeStruct((2, rows // 8, 4 * LANES), F32),
        in_specs=[SMEM, SMEM, HBM, HBM, HBM, HBM],
        out_specs=HBM,
        scratch_shapes=[
            pltpu.VMEM((2, rows // 8, 4 * LANES), F32),
            pltpu.VMEM((3 * rows, LANES), F32),
            pltpu.VMEM(table.shape, F32),
            pltpu.VMEM((2 * table.shape[0], LANES), F32),
            pltpu.VMEM((rows, LANES), F32),
            pltpu.VMEM((rows, LANES), F32),
            pltpu.SemaphoreType.DMA((8,)),
        ],
        compiler_params=pltpu.CompilerParams(vmem_limit_bytes=24 * MIB),
        cost_estimate=estimate(9),
        name="top_translate",
    )(src, kind, own, mate, cross, table)


def leaf_kernel(
    src_hbm,
    type_hbm,
    own_hbm,
    pair_a_hbm,
    pair_b_hbm,
    table_hbm,
    out_hbm,
    out_ref,
    src_ref,
    type_ref,
    near_ref,
    tab_ref,
    leaf_ref,
    one_ref,
    two_ref,
    sem,
):
    leaves = own_hbm.shape[1]
    reach = pair_a_hbm.shape[1]
    chunks = own_hbm.shape[2] // LANES
    size = 2 * chunks
    pitch = 2 * size + PAD
    side = lax.axis_index("dir") % 2
    after = reach + leaves
    place_a = pl.multiple_of((1 - side) * after, 8)
    place_b = pl.multiple_of(side * after, 8)
    gets = [
        pltpu.make_async_copy(source, target, sem.at[i])
        for i, (source, target) in enumerate(
            (
                (own_hbm, near_ref.at[:, reach:after, :]),
                (pair_a_hbm, near_ref.at[:, pl.ds(place_a, reach), :]),
                (pair_b_hbm, near_ref.at[:, pl.ds(place_b, reach), :]),
                (src_hbm, src_ref),
                (type_hbm, type_ref),
            )
        )
    ]
    share = table_hbm.shape[0] // 4
    tables = [
        pltpu.make_async_copy(
            table_hbm.at[q * share:(q + 1) * share, :], tab_ref.at[q * share:(q + 1) * share, :], sem.at[8 + q]
        )
        for q in range(4)
    ]
    for get in gets[:3] + tables + gets[3:]:
        get.start()
    for get in gets[:3]:
        get.wait()
    for first in range(0, near_ref.shape[1], 8):
        for c in range(chunks):
            lanes = slice(c * LANES, (c + 1) * LANES)
            real = near_ref[0, first:first + 8, lanes]
            imag = near_ref[1, first:first + 8, lanes]
            at = first * pitch + 2 * c
            leaf_ref[pl.ds(at, 8, stride=pitch), :] = real
            leaf_ref[pl.ds(at + 1, 8, stride=pitch), :] = imag
            leaf_ref[pl.ds(at + size, 8, stride=pitch), :] = imag
            leaf_ref[pl.ds(at + size + 1, 8, stride=pitch), :] = real
    for get in tables + gets[3:]:
        get.wait()
    line = size + PAD

    def body(i, carry):
        one = jnp.zeros((size, LANES), F32)
        two = jnp.zeros((size, LANES), F32)
        for j in range(src_ref.shape[0]):
            s = pl.multiple_of(src_ref[j, i], 8)
            t = pl.multiple_of(type_ref[j, i], size)
            tab = tab_ref[pl.ds(t, size), :]
            one = one + tab * leaf_ref[pl.ds(s, size), :]
            two = two + tab * leaf_ref[pl.ds(s + size, size), :]
        at = pl.ds(pl.multiple_of(i * line, 8), size)
        one_ref[at, :] = one
        two_ref[at, :] = two
        return carry

    parts = 3
    puts = []
    for q in range(parts):
        start = q * leaves // parts
        rows = slice(start, start + leaves // parts)
        lax.fori_loop(rows.start, rows.stop, body, 0)
        for first in range(rows.start, rows.stop, 8):
            for c in range(chunks):
                lanes = slice(c * LANES, (c + 1) * LANES)
                even = pl.ds(first * line + 2 * c, 8, stride=line)
                odd = pl.ds(first * line + 2 * c + 1, 8, stride=line)
                out_ref[0, first:first + 8, lanes] = one_ref[even, :] - one_ref[odd, :]
                out_ref[1, first:first + 8, lanes] = two_ref[even, :] + two_ref[odd, :]
        puts.append(pltpu.make_async_copy(out_ref.at[:, rows, :], out_hbm.at[:, rows, :], sem.at[5 + q]))
        puts[q].start()
    for put in puts:
        put.wait()


def leaf_translate(src, kind, own, pair_a, pair_b, table):
    leaves = own.shape[1]
    reach = pair_a.shape[1]
    size = 2 * own.shape[2] // LANES
    line = size + PAD
    near = leaves + 2 * reach
    return pl.pallas_call(
        leaf_kernel,
        out_shape=jax.ShapeDtypeStruct(own.shape, F32),
        in_specs=[ANY, ANY, HBM, ANY, ANY, HBM],
        out_specs=HBM,
        scratch_shapes=[
            pltpu.VMEM(own.shape, F32),
            pltpu.SMEM(src.shape, I32),
            pltpu.SMEM(kind.shape, I32),
            pltpu.VMEM((2, near, own.shape[2]), F32),
            pltpu.VMEM(table.shape, F32),
            pltpu.VMEM((near * (2 * size + PAD), LANES), F32),
            pltpu.VMEM((leaves * line, LANES), F32),
            pltpu.VMEM((leaves * line, LANES), F32),
            pltpu.SemaphoreType.DMA((12,)),
        ],
        compiler_params=pltpu.CompilerParams(vmem_limit_bytes=53 * MIB),
        cost_estimate=estimate(5),
        name="leaf_translate",
    )(src, kind, own, pair_a, pair_b, table)


def interleaved(table):
    types = table.shape[1]
    view = table.reshape(2, types, -1, LANES)
    return view.transpose(1, 2, 0, 3).reshape(-1, LANES)


def per_device(
    leaf_pattern,
    leaf_parent,
    octant,
    interp_theta,
    interp_phi,
    shift_angle,
    near_src,
    near_type,
    leaf_transfer,
    inter_src,
    inter_type,
    top_transfer,
):
    leaves = leaf_pattern.shape[1]
    dirs = lax.axis_size("dir")
    groups = lax.axis_size("box")
    box = lax.axis_index("box")
    parents, edge_b, edge_a = aggregate(
        leaf_pattern, octant, leaf_parent, interp_theta.T, interp_phi.T, shift_angle, dirs
    )
    directed = lax.all_to_all(parents, "dir", split_axis=0, concat_axis=0)
    count = dirs * groups
    pair_a = lax.ppermute(edge_a, ("box", "dir"), [(i, i ^ 1) for i in range(count)])
    pair_b = lax.ppermute(edge_b, ("box", "dir"), [(i, ((i + 1) ^ 1) - 1) for i in range(1, count - 1)])

    own = directed.reshape(-1, LANES)
    boxes = inter_src.shape[0]
    mate = lax.ppermute(own, "box", [(i, i ^ 1) for i in range(groups)])
    cross = lax.ppermute(own, "box", [(i, ((i + 1) ^ 1) - 1) for i in range(1, groups - 1)])
    src = inter_src.T
    group = src // boxes
    place = jnp.where(group == box, 0, jnp.where(group == (box ^ 1), boxes, 2 * boxes)) + src % boxes
    top_src = (place * 8).reshape(-1)
    top_type = (inter_type.T * 16).reshape(-1)
    incoming = top_translate(top_src, top_type, own, mate, cross, interleaved(top_transfer))

    size = 2 * leaf_pattern.shape[2] // LANES
    first_leaf = lax.axis_index(("box", "dir")) * leaves
    leaf_src = (near_src.T - (first_leaf - REACH)) * (2 * size + PAD)
    leaf_incoming = leaf_translate(
        leaf_src, near_type.T * size, leaf_pattern, pair_a, pair_b, interleaved(leaf_transfer)
    )
    return (incoming, leaf_incoming)


def solution(mesh):
    return jax.shard_map(
        per_device,
        mesh=mesh,
        in_specs=(
            P(None, ("box", "dir"), None),
            P(("box", "dir"), None),
            P(("box", "dir")),
            P(),
            P(),
            P(),
            P(("box", "dir"), None),
            P(("box", "dir"), None),
            P(),
            P("box", None),
            P("box", None),
            P(None, None, "dir"),
        ),
        out_specs=(P(None, "box", "dir"), P(None, ("box", "dir"), None)),
        check_vma=False,
    )
```
